256 devices in a mesh: vir: 64 (over y_hi, x, z), occ: 4 (over y_lo, core).
Axes of the slice: x: 4, y: 4 (y_hi: 2, y_lo: 2; y = y_hi * 2 + y_lo), z: 8, core: 2. Of those that a mesh axis runs over, the one named last changes fastest.
Arguments:
- l3_tiles: bfloat16 [64, 512, 128, 128], P('occ', 'vir'), may hold values from -6 to 6
- active: int32 [64, 512], P('occ', 'vir'), may hold values 0 or 1
- panels: bfloat16 [512, 128, 128], P('vir'), may hold values from -0.5 to 0.5
- coupling: float32 [512, 24], P('vir'), may hold values from -1.25 to 1.25
Outputs:
- r3_tiles: bfloat16 [64, 512, 128, 128], P('occ', 'vir')
- l2_block: bfloat16 [16, 128, 128], P('occ', 'vir')
The draws below stay inside these ranges and needn't reach their ends.
All inputs are finite; a program needn't handle non-finite values. No bound on the sum of `active` on one device may be relied on, other than what follows from the above.
Results may differ from the reference program's by a relative error of at most 0.0049.
Values may be sent and summed in bfloat16 or wider, within the bound.
No kernel may reach another device: no remote copies, remote signals or barrier semaphores. Data moves between devices by JAX's collectives and lax.ppermute only.
A program may use at most 64 MiB of HBM per device.

```python
import jax
import jax.numpy as jnp
from jax import lax

TW = 128
PAIR_DEV = 8
TRI_DEV = 16
PAIRS = 512
TRIPLES = 64
N_VIR = 64
N_OCC = 4


def with_ends(result, stream_key, low, largest):
    index_at = [jax.random.randint(jax.random.fold_in(stream_key, axis), (), 0, length) for axis, length in enumerate(result.shape)]
    widest = result.shape.index(max(result.shape))
    neighbour = index_at[:widest] + [(index_at[widest] + 1) % result.shape[widest]] + index_at[widest + 1:]
    return result.at[tuple(index_at)].set(low).at[tuple(neighbour)].set(largest)


def levels(key, shape, shards, low, largest):
    gain, own = 1.0, jax.random.fold_in(key, 6)
    for axis_at, blocks in shards:
        steps = jnp.exp(jax.random.uniform(jax.random.fold_in(own, axis_at), (blocks,), jnp.float32, low / len(shards), largest / len(shards)))
        gain = gain * jnp.repeat(steps, shape[axis_at] // blocks).reshape([-1 if axis == axis_at else 1 for axis in range(len(shape))])
    return gain


def gaussian(rng, dims, spread, limit, split=(), dtype=jnp.bfloat16):
    loudness = levels(rng, dims, split, -0.22, 0.18) if split else 1.0
    drawn = jax.random.normal(rng, dims, jnp.float32) * spread * loudness
    return jnp.minimum(jnp.maximum(drawn, -limit), limit).astype(dtype)


def setup_inputs(seed: int = 0) -> dict:
    streams_of = jax.random.split(jax.random.key(seed), 5)
    return {
        "l3_tiles": gaussian(streams_of[0], (TRIPLES, PAIRS, TW, TW), 1.0, 6.0, ((0, 4), (1, 64))),
        "active": with_ends((jax.random.randint(streams_of[1], (TRIPLES, PAIRS), 0, 3) < 2).astype(jnp.int32), jax.random.fold_in(streams_of[1], 1), 0, 1),
        "panels": gaussian(streams_of[2], (PAIRS, TW, TW), TW ** -0.5, 0.5, ((0, 64),)),
        "coupling": gaussian(streams_of[3], (PAIRS, 3 * PAIR_DEV), (3 * PAIR_DEV) ** -0.5, 1.25, ((0, 64),), jnp.float32),
    }


def reference(l3_tiles, active, panels, coupling):
    blocks = panels.astype(jnp.float32).reshape(N_VIR, PAIR_DEV, TW * TW)
    before = jnp.roll(blocks, 1, axis=0)
    after = jnp.roll(blocks, -1, axis=0)
    window = jnp.concatenate([before, blocks, after], axis=1)
    weights = coupling.reshape(N_VIR, PAIR_DEV, 3 * PAIR_DEV)
    combined = jnp.einsum('vpj,vjx->vpx', weights, window, precision=lax.Precision.HIGHEST)
    combined = combined.reshape(PAIRS, TW, TW).astype(jnp.bfloat16)
    pan32 = panels.astype(jnp.float32)
    combined_float32 = combined.astype(jnp.float32)
    mask = active.astype(jnp.float32)

    def per_triple(items):
        tiles, row = items
        masked_rows = tiles.astype(jnp.float32) * row[:, None, None]
        return jnp.einsum('pab,pbc->ac', masked_rows, pan32)
    summed = lax.map(per_triple, (l3_tiles, mask))
    meansq = lax.optimization_barrier(jnp.mean(summed * summed, axis=(1, 2)))
    normed_values = (summed * lax.rsqrt(meansq + 1e-05)[:, None, None]).astype(jnp.bfloat16)

    def residual(items):
        tiles, row, norm_tile_rows = items
        masked_rows = tiles.astype(jnp.float32) * row[:, None, None]
        direct = jnp.einsum('pab,pbc->pac', masked_rows, combined_float32)
        returned_rows = jnp.einsum('ac,pdc->pad', norm_tile_rows.astype(jnp.float32), pan32)
        return (direct + row[:, None, None] * returned_rows).astype(jnp.bfloat16)
    r3_tiles = lax.map(residual, (l3_tiles, mask, normed_values))
    grouped_rows = lax.optimization_barrier(jnp.sum(summed.reshape(N_OCC, TRI_DEV, TW, TW), axis=0))
    l2_block = (grouped_rows / jnp.sqrt(jnp.float32(PAIRS))).astype(jnp.bfloat16)
    return (r3_tiles, l2_block)
```

```python
import functools

import jax
import jax.numpy as jnp
from jax import lax
from jax.experimental import pallas as pl
from jax.experimental.pallas import tpu as pltpu
from jax.sharding import PartitionSpec as P

VMEM_LIMIT = 40 * 1024 * 1024


def partial_kernel(active_ref, l3_ref, panels_ref, out_ref):
    block, pairs, width, _ = l3_ref.shape
    first = pl.program_id(0) * block
    weights = panels_ref[...].reshape(pairs * width, width)
    rows = []
    for t in range(block):
        tiles = [
            l3_ref[t, p] * active_ref[first + t, p].astype(jnp.float32).astype(jnp.bfloat16)
            for p in range(pairs)
        ]
        rows.append(jnp.concatenate(tiles, axis=1))
    lhs = jnp.concatenate(rows, axis=0)
    out_ref[...] = jnp.dot(lhs, weights, preferred_element_type=jnp.float32).astype(jnp.bfloat16)


def partial_sums(active, l3, panels, block=4):
    triples, pairs, width, _ = l3.shape
    return pl.pallas_call(
        partial_kernel,
        grid=(triples // block,),
        in_specs=[
            pl.BlockSpec(memory_space=pltpu.SMEM),
            pl.BlockSpec((block, pairs, width, width), lambda i: (i, 0, 0, 0)),
            pl.BlockSpec((pairs, width, width), lambda i: (0, 0, 0)),
        ],
        out_specs=pl.BlockSpec((block * width, width), lambda i: (i, 0)),
        out_shape=jax.ShapeDtypeStruct((triples * width, width), jnp.bfloat16),
        compiler_params=pltpu.CompilerParams(vmem_limit_bytes=VMEM_LIMIT),
        cost_estimate=pl.CostEstimate(
            flops=2 * triples * pairs * width**3, bytes_accessed=l3.size * 2, transcendentals=0
        ),
        name="partial_sums",
    )(active, l3, panels)


def total_kernel(parts_ref, out_ref):
    count = parts_ref.shape[0]
    total = parts_ref[0].astype(jnp.float32)
    for i in range(1, count):
        total = total + parts_ref[i].astype(jnp.float32)
    rounded = total.astype(jnp.bfloat16)
    for i in range(count):
        out_ref[i] = rounded


def total_copies(parts):
    return pl.pallas_call(
        total_kernel,
        in_specs=[pl.BlockSpec(memory_space=pltpu.VMEM)],
        out_specs=pl.BlockSpec(memory_space=pltpu.VMEM),
        out_shape=jax.ShapeDtypeStruct(parts.shape, jnp.bfloat16),
        cost_estimate=pl.CostEstimate(flops=parts.size, bytes_accessed=parts.size * 4, transcendentals=0),
        name="total_copies",
    )(parts)


def final_kernel(active_ref, l3_ref, summed_ref, combined_ref, panels_ref, out_ref, weights):
    block, pairs, width, _ = l3_ref.shape
    first = pl.program_id(0) * block

    @pl.when(pl.program_id(0) == 0)
    def _():
        for p in range(pairs):
            weights[p, :width] = combined_ref[p]
            weights[p, width:] = panels_ref[p].T

    normed = []
    for t in range(block):
        summed = summed_ref[t].astype(jnp.float32)
        meansq = jnp.sum(summed * summed) / (width * width)
        normed.append((summed * lax.rsqrt(meansq + 1e-05)).astype(jnp.bfloat16))
    for p in range(pairs):
        rows = []
        for t in range(block):
            mask = active_ref[first + t, p].astype(jnp.float32).astype(jnp.bfloat16)
            rows.append(jnp.concatenate([l3_ref[t, p] * mask, normed[t] * mask], axis=1))
        lhs = jnp.concatenate(rows, axis=0)
        tile = jnp.dot(lhs, weights[p], preferred_element_type=jnp.float32)
        out_ref[:, p] = tile.astype(jnp.bfloat16).reshape(block, width, width)


def residual(active, l3, summed, combined, panels, block=4):
    triples, pairs, width, _ = l3.shape
    return pl.pallas_call(
        final_kernel,
        grid=(triples // block,),
        in_specs=[
            pl.BlockSpec(memory_space=pltpu.SMEM),
            pl.BlockSpec((block, pairs, width, width), lambda i: (i, 0, 0, 0)),
            pl.BlockSpec((block, width, width), lambda i: (i, 0, 0)),
            pl.BlockSpec((pairs, width, width), lambda i: (0, 0, 0)),
            pl.BlockSpec((pairs, width, width), lambda i: (0, 0, 0)),
        ],
        out_specs=pl.BlockSpec((block, pairs, width, width), lambda i: (i, 0, 0, 0)),
        out_shape=jax.ShapeDtypeStruct(l3.shape, jnp.bfloat16),
        scratch_shapes=[pltpu.VMEM((pairs, 2 * width, width), jnp.bfloat16)],
        compiler_params=pltpu.CompilerParams(vmem_limit_bytes=VMEM_LIMIT),
        cost_estimate=pl.CostEstimate(
            flops=4 * triples * pairs * width**3, bytes_accessed=l3.size * 4, transcendentals=0
        ),
        name="residual",
    )(active, l3, summed, combined, panels)


def shards(l3_tiles, active, panels, coupling):
    triples, pairs, width, _ = l3_tiles.shape
    vir_count, occ_count = lax.axis_size("vir"), lax.axis_size("occ")
    rows = width // vir_count
    up = [(i, (i + 1) % vir_count) for i in range(vir_count)]
    down = [(j, i) for i, j in up]
    before = lax.ppermute(panels, "vir", up)
    after = lax.ppermute(panels, "vir", down)

    partial = partial_sums(active, l3_tiles, panels)
    parts = lax.all_to_all(partial.reshape(vir_count, -1, width), "vir", 0, 0, tiled=True)
    copies = total_copies(parts)
    summed = lax.all_to_all(copies, "vir", 0, 0, tiled=True).reshape(triples, width, width)

    window = jnp.concatenate([before, panels, after], axis=0)
    flat_window = window.reshape(3 * pairs, width * width).astype(jnp.float32)
    combined = jnp.dot(coupling, flat_window, precision=lax.Precision.HIGHEST)
    combined = combined.reshape(pairs, width, width).astype(jnp.bfloat16)

    local = lax.dynamic_slice_in_dim(summed, lax.axis_index("vir") * rows, rows, 1)
    local = local.astype(jnp.float32).reshape(occ_count, triples // occ_count, rows, width)
    groups = lax.all_to_all(local, "occ", 0, 0, tiled=True)
    r3_tiles = residual(active, l3_tiles, summed, combined, panels)
    total_pairs = pairs * vir_count
    l2_block = (jnp.sum(groups, axis=0) / jnp.sqrt(jnp.float32(total_pairs))).astype(jnp.bfloat16)
    return (r3_tiles, l2_block)


def solution(mesh):
    return jax.shard_map(
        shards,
        mesh=mesh,
        in_specs=(
            P("occ", "vir", None, None),
            P("occ", "vir"),
            P("vir", None, None),
            P("vir", None),
        ),
        out_specs=(P("occ", "vir", None, None), P("occ", "vir", None)),
        check_vma=False,
    )
```

```python
import jax
import jax.numpy as jnp
from jax import lax
from jax.experimental import pallas as pl
from jax.experimental.pallas import tpu as pltpu
from jax.sharding import Mesh
from jax.sharding import PartitionSpec as P

MEDIUM = 16 * 1024 * 1024
LARGE = 60 * 1024 * 1024
SMALL = 4 * 1024 * 1024
VIR = ("yh", "x", "zh", "zl")
OCC = ("yl", "core")
NEAR = ("yh", "x", "zl")
EXTRA = 16


def params(limit):
    return pltpu.CompilerParams(vmem_limit_bytes=limit)


def whole(count):
    return [pl.BlockSpec(memory_space=pltpu.VMEM)] * count


def partial_kernel(flags_ref, l3_ref, panels_ref, out_ref, tiles_ref, held_ref, sems, *, block):
    triples, pairs, width, _ = l3_ref.shape
    loads = [
        pltpu.make_async_copy(l3_ref.at[t], tiles_ref.at[t], sems.at[t]) for t in range(triples)
    ]
    fetch = pltpu.make_async_copy(panels_ref, held_ref, sems.at[triples])
    fetch.start()
    for load in loads[: triples // 2]:
        load.start()
    fetch.wait()
    for load in loads[triples // 2 :]:
        load.start()
    weights = held_ref[...].reshape(pairs * width, width)
    for first in range(0, triples, block):
        rows = []
        for t in range(first, first + block):
            loads[t].wait()
            tiles = [
                tiles_ref[t, p] * flags_ref[p, t].astype(jnp.float32).astype(jnp.bfloat16)
                for p in range(pairs)
            ]
            rows.append(jnp.concatenate(tiles, axis=1))
        lhs = jnp.concatenate(rows, axis=0)
        sums = jnp.dot(lhs, weights, preferred_element_type=jnp.float32)
        out_ref[first * width : (first + block) * width] = sums.astype(jnp.bfloat16)


def partial_sums(flags, l3, panels, block=2):
    triples, pairs, width, _ = l3.shape

    def kernel(*refs):
        partial_kernel(*refs, block=block)

    return pl.pallas_call(
        kernel,
        in_specs=[
            pl.BlockSpec(memory_space=pltpu.SMEM),
            pl.BlockSpec(memory_space=pltpu.HBM),
            pl.BlockSpec(memory_space=pltpu.HBM),
        ],
        out_specs=whole(1)[0],
        out_shape=jax.ShapeDtypeStruct((triples * width, width), jnp.bfloat16),
        scratch_shapes=[
            pltpu.VMEM(l3.shape, jnp.bfloat16),
            pltpu.VMEM(panels.shape, jnp.bfloat16),
            pltpu.SemaphoreType.DMA((triples + 1,)),
        ],
        compiler_params=params(LARGE),
        cost_estimate=pl.CostEstimate(
            flops=2 * triples * pairs * width**3, bytes_accessed=l3.size * 2, transcendentals=0
        ),
        name="partial_sums",
    )(flags, l3, panels)


def add_up(parts_ref):
    total = parts_ref[0].astype(jnp.float32)
    for i in range(1, parts_ref.shape[0]):
        total = total + parts_ref[i].astype(jnp.float32)
    return total


def near_kernel(parts_ref, out_ref):
    rounded = add_up(parts_ref).astype(jnp.bfloat16)
    for i in range(out_ref.shape[0]):
        out_ref[i] = rounded


def near_sums(parts, count):
    return pl.pallas_call(
        near_kernel,
        in_specs=whole(1),
        out_specs=whole(1)[0],
        out_shape=jax.ShapeDtypeStruct((count, *parts.shape[1:]), jnp.bfloat16),
        compiler_params=params(SMALL),
        cost_estimate=pl.CostEstimate(flops=parts.size, bytes_accessed=parts.size * 4, transcendentals=0),
        name="near_sums",
    )(parts)


def normed_kernel(line_ref, parts_ref, out_ref, summed_ref, *, rows):
    _, chunk, width = parts_ref.shape
    count = out_ref.shape[0]
    summed_ref[...] = add_up(parts_ref)
    for first in range(0, chunk, width):
        tile = summed_ref[first : first + width]
        meansq = jnp.sum(tile * tile) / (width * width)
        normed = (tile * lax.rsqrt(meansq + 1e-05)).astype(jnp.bfloat16)
        for i in range(count):
            out_ref[i, first : first + width] = normed
    far = parts_ref.shape[0]
    for i in range(count):
        start = (i // 2 * 2 * far + line_ref[0] * 2 + i % 2) * rows
        own = [summed_ref[pl.ds(first + start, rows)] for first in range(0, chunk, width)]
        own = jnp.concatenate(own, axis=0)
        high = own.astype(jnp.bfloat16).astype(jnp.float32)
        zeros = jnp.zeros((EXTRA - 2 * own.shape[0], width), jnp.float32)
        pieces = jnp.concatenate([high, own - high, zeros], axis=0)
        out_ref[i, chunk:] = pieces.astype(jnp.bfloat16)


def normed_copies(parts, line, rows, count):
    _, chunk, width = parts.shape

    def kernel(*refs):
        normed_kernel(*refs, rows=rows)

    return pl.pallas_call(
        kernel,
        in_specs=[pl.BlockSpec(memory_space=pltpu.SMEM), *whole(1)],
        out_specs=whole(1)[0],
        out_shape=jax.ShapeDtypeStruct((count, chunk + EXTRA, width), jnp.bfloat16),
        scratch_shapes=[pltpu.VMEM((chunk, width), jnp.float32)],
        compiler_params=params(SMALL),
        cost_estimate=pl.CostEstimate(flops=parts.size, bytes_accessed=parts.size * 4, transcendentals=0),
        name="normed_copies",
    )(line, parts)


def weights_kernel(combined_ref, panels_ref, out_ref):
    pairs, width, _ = panels_ref.shape
    for p in range(pairs):
        out_ref[p, :width] = combined_ref[p]
        out_ref[p, width:] = panels_ref[p].T


def stacked_weights(combined, panels):
    pairs, width, _ = panels.shape
    return pl.pallas_call(
        weights_kernel,
        in_specs=whole(2),
        out_specs=whole(1)[0],
        out_shape=jax.ShapeDtypeStruct((pairs, 2 * width, width), jnp.bfloat16),
        compiler_params=params(SMALL),
        cost_estimate=pl.CostEstimate(flops=0, bytes_accessed=panels.size * 8, transcendentals=0),
        name="stacked_weights",
    )(combined, panels)


def final_kernel(flags_ref, l3_ref, normed_ref, weights_ref, r3_ref, out_ref, sems, *, block):
    triples, pairs, width, _ = l3_ref.shape
    held = triples // normed_ref.shape[0]
    stores = [pltpu.make_async_copy(out_ref.at[t], r3_ref.at[t], sems.at[t]) for t in range(triples)]
    for first in range(0, triples, block):
        here = range(first, first + block)
        normed = [normed_ref[t // held, t % held * width : (t % held + 1) * width] for t in here]
        for p in range(pairs):
            lhs = [jnp.concatenate([l3_ref[t, p], normed[t - first]], axis=1) for t in here]
            lhs = jnp.concatenate(lhs, axis=0)
            sums = jnp.dot(lhs, weights_ref[p], preferred_element_type=jnp.float32)
            for t in here:
                mask = flags_ref[p, t].astype(jnp.float32)
                tile = sums[(t - first) * width : (t - first + 1) * width] * mask
                out_ref[t, p] = tile.astype(jnp.bfloat16)
        for t in here:
            stores[t].start()
    for store in stores:
        store.wait()


def residual(flags, l3, normed, weights, block=2):
    triples, pairs, width, _ = l3.shape

    def kernel(*refs):
        final_kernel(*refs, block=block)

    return pl.pallas_call(
        kernel,
        in_specs=[pl.BlockSpec(memory_space=pltpu.SMEM), *whole(3)],
        out_specs=pl.BlockSpec(memory_space=pltpu.HBM),
        out_shape=jax.ShapeDtypeStruct(l3.shape, jnp.bfloat16),
        scratch_shapes=[
            pltpu.VMEM(l3.shape, jnp.bfloat16),
            pltpu.SemaphoreType.DMA((triples,)),
        ],
        compiler_params=params(MEDIUM),
        cost_estimate=pl.CostEstimate(
            flops=4 * triples * pairs * width**3, bytes_accessed=l3.size * 4, transcendentals=0
        ),
        name="residual",
    )(flags, l3, normed, weights)


def occ_sum(blocks):
    count = blocks.shape[0]
    me = lax.axis_index(OCC)
    total = lax.dynamic_index_in_dim(blocks, me, 0, keepdims=False)
    for step in range(1, count):
        sent = lax.dynamic_index_in_dim(blocks, me ^ step, 0, keepdims=False)
        total = total + lax.ppermute(sent, OCC, [(i, i ^ step) for i in range(count)])
    return total


def halo(panels):
    count = lax.axis_size(VIR)
    ring = [((v, 0), ((v + 1) % count, 0)) for v in range(count)]
    ring += [((v, 1), ((v - 1) % count, 1)) for v in range(count)]
    pairs = [(2 * v + c, 2 * w + d) for (v, c), (w, d) in ring]
    mine = lax.ppermute(panels, (*VIR, "core"), pairs)
    other = lax.ppermute(mine, "core", [(0, 1), (1, 0)])
    first = lax.axis_index("core") == 0
    return jnp.where(first, mine, other), jnp.where(first, other, mine)


def shards(l3_tiles, active, panels, coupling):
    triples, pairs, width, _ = l3_tiles.shape
    vir_count, occ_count = lax.axis_size(VIR), lax.axis_size(OCC)
    near, far = lax.axis_size(NEAR), lax.axis_size("zh")
    rows = width // vir_count
    flags = active.T
    partial = partial_sums(flags, l3_tiles, panels)
    before, after = halo(panels)
    parts = lax.all_to_all(partial.reshape(near, -1, width), NEAR, 0, 0, tiled=True)

    window = jnp.concatenate([before, panels, after], axis=0)
    flat_window = window.reshape(3 * pairs, width * width).astype(jnp.float32)
    combined = jnp.dot(coupling, flat_window, precision=lax.Precision.HIGHEST)
    combined = combined.reshape(pairs, width, width).astype(jnp.bfloat16)
    parts, combined = lax.optimization_barrier((parts, combined))

    copies, combined = lax.optimization_barrier((near_sums(parts, far), combined))
    parts = lax.all_to_all(copies, "zh", 0, 0, tiled=True)
    weights = stacked_weights(combined, panels)
    parts, weights = lax.optimization_barrier((parts, weights))

    line = lax.axis_index("zh").reshape(1)
    copies = normed_copies(parts, line, rows, near)
    gathered = lax.all_to_all(copies, NEAR, 0, 0, tiled=True)
    high_low = gathered[:, -EXTRA:][:, : 2 * triples // near * rows].astype(jnp.float32)
    high_low = high_low.reshape(near, 2, triples // near, rows, width)
    local = (high_low[:, 0] + high_low[:, 1]).reshape(occ_count, triples // occ_count, rows, width)
    total = occ_sum(local)
    r3_tiles = residual(flags, l3_tiles, gathered, weights)
    l2_block = (total / jnp.sqrt(jnp.float32(pairs * vir_count))).astype(jnp.bfloat16)
    return (r3_tiles, l2_block)


def solution(mesh):
    vir_count, occ_count = mesh.devices.shape
    split = mesh.devices.reshape(2, 4, vir_count // 16, 2, occ_count // 2, 2)
    return jax.shard_map(
        shards,
        mesh=Mesh(split, (*VIR, *OCC)),
        in_specs=(
            P(OCC, VIR, None, None),
            P(OCC, VIR),
            P(VIR, None, None),
            P(VIR, None),
        ),
        out_specs=(P(OCC, VIR, None, None), P(OCC, VIR, None)),
        check_vma=False,
    )
```

```python
import jax
import jax.numpy as jnp
from jax import lax
from jax.experimental import pallas as pl
from jax.experimental.pallas import tpu as pltpu
from jax.sharding import Mesh
from jax.sharding import PartitionSpec as P

MEDIUM = 16 * 1024 * 1024
LARGE = 60 * 1024 * 1024
SMALL = 4 * 1024 * 1024
VIR = ("yh", "x", "zh", "zl")
OCC = ("yl", "core")
NEAR = ("yh", "x", "zl")
EXTRA = 16


def params(limit):
    return pltpu.CompilerParams(vmem_limit_bytes=limit)


def whole(count):
    return [pl.BlockSpec(memory_space=pltpu.VMEM)] * count


def partial_kernel(flags_ref, l3_ref, panels_ref, out_ref, tiles_ref, held_ref, sems, *, block):
    triples, pairs, width, _ = l3_ref.shape
    half = triples // 2
    fetch = pltpu.make_async_copy(panels_ref, held_ref, sems.at[0])
    fetch.start()
    loads = []
    for i in range(2):
        here = pl.ds(i * half, half)
        loads.append(pltpu.make_async_copy(l3_ref.at[here], tiles_ref.at[here], sems.at[i + 1]))
        loads[i].start()
    fetch.wait()
    weights = held_ref[...].reshape(pairs * width, width)
    for first in range(0, triples, block):
        if first % half == 0:
            loads[first // half].wait()
        rows = []
        for t in range(first, first + block):
            tiles = [
                tiles_ref[t, p] * flags_ref[p, t].astype(jnp.float32).astype(jnp.bfloat16)
                for p in range(pairs)
            ]
            rows.append(jnp.concatenate(tiles, axis=1))
        lhs = jnp.concatenate(rows, axis=0)
        sums = jnp.dot(lhs, weights, preferred_element_type=jnp.float32)
        out_ref[first * width : (first + block) * width] = sums.astype(jnp.bfloat16)


def partial_sums(flags, l3, panels, block=2):
    triples, pairs, width, _ = l3.shape

    def kernel(*refs):
        partial_kernel(*refs, block=block)

    return pl.pallas_call(
        kernel,
        in_specs=[
            pl.BlockSpec(memory_space=pltpu.SMEM),
            pl.BlockSpec(memory_space=pltpu.HBM),
            pl.BlockSpec(memory_space=pltpu.HBM),
        ],
        out_specs=whole(1)[0],
        out_shape=jax.ShapeDtypeStruct((triples * width, width), jnp.bfloat16),
        scratch_shapes=[
            pltpu.VMEM(l3.shape, jnp.bfloat16),
            pltpu.VMEM(panels.shape, jnp.bfloat16),
            pltpu.SemaphoreType.DMA((3,)),
        ],
        compiler_params=params(LARGE),
        cost_estimate=pl.CostEstimate(
            flops=2 * triples * pairs * width**3, bytes_accessed=l3.size * 2, transcendentals=0
        ),
        name="partial_sums",
    )(flags, l3, panels)


def add_up(parts):
    total = parts[0][...].astype(jnp.float32)
    for part in parts[1:]:
        total = total + part[...].astype(jnp.float32)
    return total


def near_kernel(parts_ref, out_ref):
    parts = [parts_ref.at[i] for i in range(parts_ref.shape[0])]
    out_ref[...] = add_up(parts).astype(jnp.bfloat16)


def near_sums(parts):
    return pl.pallas_call(
        near_kernel,
        in_specs=whole(1),
        out_specs=whole(1)[0],
        out_shape=jax.ShapeDtypeStruct(parts.shape[1:], jnp.bfloat16),
        compiler_params=params(SMALL),
        cost_estimate=pl.CostEstimate(flops=parts.size, bytes_accessed=parts.size * 4, transcendentals=0),
        name="near_sums",
    )(parts)


def normed_kernel(line_ref, *refs, rows):
    *parts, out_ref, summed_ref = refs
    chunk, width = summed_ref.shape
    count = out_ref.shape[0]
    summed_ref[...] = add_up(parts)
    for first in range(0, chunk, width):
        tile = summed_ref[first : first + width]
        meansq = jnp.sum(tile * tile) / (width * width)
        normed = (tile * lax.rsqrt(meansq + 1e-05)).astype(jnp.bfloat16)
        for i in range(count):
            out_ref[i, first : first + width] = normed
    far = len(parts)
    for i in range(count):
        start = (i // 2 * 2 * far + line_ref[0] * 2 + i % 2) * rows
        own = [summed_ref[pl.ds(first + start, rows)] for first in range(0, chunk, width)]
        own = jnp.concatenate(own, axis=0)
        high = own.astype(jnp.bfloat16).astype(jnp.float32)
        zeros = jnp.zeros((EXTRA - 2 * own.shape[0], width), jnp.float32)
        pieces = jnp.concatenate([high, own - high, zeros], axis=0)
        out_ref[i, chunk:] = pieces.astype(jnp.bfloat16)


def normed_copies(parts, line, rows, count):
    chunk, width = parts[0].shape

    def kernel(*refs):
        normed_kernel(*refs, rows=rows)

    return pl.pallas_call(
        kernel,
        in_specs=[pl.BlockSpec(memory_space=pltpu.SMEM), *whole(len(parts))],
        out_specs=whole(1)[0],
        out_shape=jax.ShapeDtypeStruct((count, chunk + EXTRA, width), jnp.bfloat16),
        scratch_shapes=[pltpu.VMEM((chunk, width), jnp.float32)],
        compiler_params=params(SMALL),
        cost_estimate=pl.CostEstimate(
            flops=4 * chunk * width, bytes_accessed=2 * count * chunk * width, transcendentals=0
        ),
        name="normed_copies",
    )(line, *parts)


def weights_kernel(l3_ref, combined_ref, panels_ref, out_ref):
    del l3_ref
    pairs, width, _ = panels_ref.shape
    for p in range(pairs):
        out_ref[p, :width] = combined_ref[p]
        out_ref[p, width:] = panels_ref[p].T


def stacked_weights(l3, combined, panels):
    pairs, width, _ = panels.shape
    return pl.pallas_call(
        weights_kernel,
        in_specs=whole(3),
        out_specs=whole(1)[0],
        out_shape=jax.ShapeDtypeStruct((pairs, 2 * width, width), jnp.bfloat16),
        compiler_params=params(SMALL),
        cost_estimate=pl.CostEstimate(flops=0, bytes_accessed=panels.size * 8, transcendentals=0),
        name="stacked_weights",
    )(l3, combined, panels)


def final_kernel(flags_ref, l3_ref, normed_ref, weights_ref, r3_ref, out_ref, sems, *, block):
    triples, pairs, width, _ = l3_ref.shape
    held = triples // normed_ref.shape[0]
    stores = [pltpu.make_async_copy(out_ref.at[t], r3_ref.at[t], sems.at[t]) for t in range(triples)]
    for first in range(0, triples, block):
        here = range(first, first + block)
        normed = [normed_ref[t // held, t % held * width : (t % held + 1) * width] for t in here]
        for p in range(pairs):
            lhs = [jnp.concatenate([l3_ref[t, p], normed[t - first]], axis=1) for t in here]
            lhs = jnp.concatenate(lhs, axis=0)
            sums = jnp.dot(lhs, weights_ref[p], preferred_element_type=jnp.float32)
            for t in here:
                mask = flags_ref[p, t].astype(jnp.float32)
                tile = sums[(t - first) * width : (t - first + 1) * width] * mask
                out_ref[t, p] = tile.astype(jnp.bfloat16)
        for t in here:
            stores[t].start()
    for store in stores:
        store.wait()


def residual(flags, l3, normed, weights, block=2):
    triples, pairs, width, _ = l3.shape

    def kernel(*refs):
        final_kernel(*refs, block=block)

    return pl.pallas_call(
        kernel,
        in_specs=[pl.BlockSpec(memory_space=pltpu.SMEM), *whole(3)],
        out_specs=pl.BlockSpec(memory_space=pltpu.HBM),
        out_shape=jax.ShapeDtypeStruct(l3.shape, jnp.bfloat16),
        scratch_shapes=[
            pltpu.VMEM(l3.shape, jnp.bfloat16),
            pltpu.SemaphoreType.DMA((triples,)),
        ],
        compiler_params=params(MEDIUM),
        cost_estimate=pl.CostEstimate(
            flops=4 * triples * pairs * width**3, bytes_accessed=l3.size * 4, transcendentals=0
        ),
        name="residual",
    )(flags, l3, normed, weights)


def own_indices():
    me = lax.axis_index(OCC).astype(jnp.uint32)
    return [me ^ jnp.uint32(step) for step in range(lax.axis_size(OCC))]


def occ_sum(blocks, indices):
    count = blocks.shape[0]
    zero = jnp.uint32(0)
    total = None
    for step, index in enumerate(indices):
        starts = (index, *[zero] * (blocks.ndim - 1))
        block = lax.dynamic_slice(blocks, starts, (1, *blocks.shape[1:]))[0]
        if step:
            block = lax.ppermute(block, OCC, [(i, i ^ step) for i in range(count)])
        total = block if total is None else total + block
    return total


def halo(panels):
    count = lax.axis_size(VIR)
    ring = [((v, 0), ((v + 1) % count, 0)) for v in range(count)]
    ring += [((v, 1), ((v - 1) % count, 1)) for v in range(count)]
    pairs = [(2 * v + c, 2 * w + d) for (v, c), (w, d) in ring]
    mine = lax.ppermute(panels, (*VIR, "core"), pairs)
    other = lax.ppermute(mine, "core", [(0, 1), (1, 0)])
    first = lax.axis_index("core") == 0
    return jnp.where(first, mine, other), jnp.where(first, other, mine)


def shards(l3_tiles, active, panels, coupling):
    triples, pairs, width, _ = l3_tiles.shape
    vir_count, occ_count = lax.axis_size(VIR), lax.axis_size(OCC)
    near, far = lax.axis_size(NEAR), lax.axis_size("zh")
    rows = width // vir_count
    flags = active.T
    partial = partial_sums(flags, l3_tiles, panels)
    before, after = halo(panels)
    parts = lax.all_to_all(partial.reshape(near, -1, width), NEAR, 0, 0, tiled=True)

    window = jnp.concatenate([before, panels, after], axis=0)
    flat_window = window.reshape(3 * pairs, width * width).astype(jnp.float32)
    combined = jnp.dot(coupling, flat_window, precision=lax.Precision.HIGHEST)
    combined = combined.reshape(pairs, width, width).astype(jnp.bfloat16)
    parts, combined = lax.optimization_barrier((parts, combined))

    part, combined = lax.optimization_barrier((near_sums(parts), combined))
    parts = [part]
    for step in range(1, far):
        parts.append(lax.ppermute(part, "zh", [(i, i ^ step) for i in range(far)]))
    weights = stacked_weights(l3_tiles, combined, panels)
    line = lax.axis_index("zh").reshape(1)
    indices = own_indices()
    parts, weights, line, indices = lax.optimization_barrier((parts, weights, line, indices))

    copies = normed_copies(parts, line, rows, near)
    gathered = lax.all_to_all(copies, NEAR, 0, 0, tiled=True)
    high_low = gathered[:, -EXTRA:][:, : 2 * triples // near * rows].astype(jnp.float32)
    high_low = high_low.reshape(near, 2, triples // near, rows, width)
    local = (high_low[:, 0] + high_low[:, 1]).reshape(occ_count, triples // occ_count, rows, width)
    total = occ_sum(local, indices)
    r3_tiles = residual(flags, l3_tiles, gathered, weights)
    l2_block = (total / jnp.sqrt(jnp.float32(pairs * vir_count))).astype(jnp.bfloat16)
    return (r3_tiles, l2_block)


def solution(mesh):
    vir_count, occ_count = mesh.devices.shape
    split = mesh.devices.reshape(2, 4, vir_count // 16, 2, occ_count // 2, 2)
    return jax.shard_map(
        shards,
        mesh=Mesh(split, (*VIR, *OCC)),
        in_specs=(
            P(OCC, VIR, None, None),
            P(OCC, VIR),
            P(VIR, None, None),
            P(VIR, None),
        ),
        out_specs=(P(OCC, VIR, None, None), P(OCC, VIR, None)),
        check_vma=False,
    )
```

```python
import jax
import jax.numpy as jnp
from jax import lax
from jax.experimental import pallas as pl
from jax.experimental.pallas import tpu as pltpu
from jax.sharding import Mesh
from jax.sharding import PartitionSpec as P

MEDIUM = 16 * 1024 * 1024
LARGE = 60 * 1024 * 1024
SMALL = 4 * 1024 * 1024
VIR = ("yh", "x", "zh", "zl")
OCC = ("yl", "core")
NEAR = ("yh", "x", "zl")
EXTRA = 16


def params(limit):
    return pltpu.CompilerParams(vmem_limit_bytes=limit)


def whole(count):
    return [pl.BlockSpec(memory_space=pltpu.VMEM)] * count


def partial_kernel(
    flags_ref, l3_ref, panels_ref, partial_ref, flags, tiles, held, out, sems, out_sems, *, block
):
    triples, pairs, width, _ = l3_ref.shape
    half = triples // 2
    fetches = [
        pltpu.make_async_copy(flags_ref, flags, sems.at[0]),
        pltpu.make_async_copy(panels_ref, held, sems.at[1]),
    ]
    loads = [
        pltpu.make_async_copy(
            l3_ref.at[pl.ds(i * half, half)], tiles.at[pl.ds(i * half, half)], sems.at[i + 2]
        )
        for i in range(2)
    ]
    for copy in (*fetches, *loads):
        copy.start()
    for copy in fetches:
        copy.wait()
    weights = held[...].reshape(pairs * width, width)
    stores = []
    for first in range(0, triples, block):
        if first % half == 0:
            loads[first // half].wait()
        rows = []
        for t in range(first, first + block):
            masked = [
                tiles[t, p] * flags[p, t].astype(jnp.float32).astype(jnp.bfloat16)
                for p in range(pairs)
            ]
            rows.append(jnp.concatenate(masked, axis=1))
        lhs = jnp.concatenate(rows, axis=0)
        sums = jnp.dot(lhs, weights, preferred_element_type=jnp.float32)
        here = pl.ds(first * width, block * width)
        out[here] = sums.astype(jnp.bfloat16)
        store = pltpu.make_async_copy(
            out.at[here], partial_ref.at[here], out_sems.at[first // block]
        )
        store.start()
        stores.append(store)
    for store in stores:
        store.wait()


def partial_sums(flags, l3, panels, block=2):
    triples, pairs, width, _ = l3.shape

    def kernel(*refs):
        partial_kernel(*refs, block=block)

    shape = (triples * width, width)
    return pl.pallas_call(
        kernel,
        in_specs=[pl.BlockSpec(memory_space=pltpu.HBM)] * 3,
        out_specs=pl.BlockSpec(memory_space=pltpu.HBM),
        out_shape=jax.ShapeDtypeStruct(shape, jnp.bfloat16),
        scratch_shapes=[
            pltpu.SMEM(flags.shape, jnp.int32),
            pltpu.VMEM(l3.shape, jnp.bfloat16),
            pltpu.VMEM(panels.shape, jnp.bfloat16),
            pltpu.VMEM(shape, jnp.bfloat16),
            pltpu.SemaphoreType.DMA((4,)),
            pltpu.SemaphoreType.DMA((triples // block,)),
        ],
        compiler_params=params(LARGE),
        cost_estimate=pl.CostEstimate(
            flops=2 * triples * pairs * width**3, bytes_accessed=l3.size * 2, transcendentals=0
        ),
        name="partial_sums",
    )(flags, l3, panels)


def add_up(parts):
    total = parts[0][...].astype(jnp.float32)
    for part in parts[1:]:
        total = total + part[...].astype(jnp.float32)
    return total


def near_kernel(parts_ref, out_ref):
    parts = [parts_ref.at[i] for i in range(parts_ref.shape[0])]
    out_ref[...] = add_up(parts).astype(jnp.bfloat16)


def near_sums(parts):
    return pl.pallas_call(
        near_kernel,
        in_specs=whole(1),
        out_specs=whole(1)[0],
        out_shape=jax.ShapeDtypeStruct(parts.shape[1:], jnp.bfloat16),
        compiler_params=params(SMALL),
        cost_estimate=pl.CostEstimate(flops=parts.size, bytes_accessed=parts.size * 4, transcendentals=0),
        name="near_sums",
    )(parts)


def normed_kernel(line_ref, *refs, rows):
    *parts, out_ref, summed_ref = refs
    chunk, width = summed_ref.shape
    count = out_ref.shape[0]
    summed_ref[...] = add_up(parts)
    for first in range(0, chunk, width):
        tile = summed_ref[first : first + width]
        meansq = jnp.sum(tile * tile) / (width * width)
        normed = (tile * lax.rsqrt(meansq + 1e-05)).astype(jnp.bfloat16)
        for i in range(count):
            out_ref[i, first : first + width] = normed
    far = len(parts)
    for i in range(count):
        start = (i // 2 * 2 * far + line_ref[0] * 2 + i % 2) * rows
        own = [summed_ref[pl.ds(first + start, rows)] for first in range(0, chunk, width)]
        own = jnp.concatenate(own, axis=0)
        high = own.astype(jnp.bfloat16).astype(jnp.float32)
        zeros = jnp.zeros((EXTRA - 2 * own.shape[0], width), jnp.float32)
        pieces = jnp.concatenate([high, own - high, zeros], axis=0)
        out_ref[i, chunk:] = pieces.astype(jnp.bfloat16)


def normed_copies(parts, line, rows, count):
    chunk, width = parts[0].shape

    def kernel(*refs):
        normed_kernel(*refs, rows=rows)

    return pl.pallas_call(
        kernel,
        in_specs=[pl.BlockSpec(memory_space=pltpu.SMEM), *whole(len(parts))],
        out_specs=whole(1)[0],
        out_shape=jax.ShapeDtypeStruct((count, chunk + EXTRA, width), jnp.bfloat16),
        scratch_shapes=[pltpu.VMEM((chunk, width), jnp.float32)],
        compiler_params=params(SMALL),
        cost_estimate=pl.CostEstimate(
            flops=4 * chunk * width, bytes_accessed=2 * count * chunk * width, transcendentals=0
        ),
        name="normed_copies",
    )(line, *parts)


def weights_kernel(l3_ref, combined_ref, panels_ref, out_ref):
    del l3_ref
    pairs, width, _ = panels_ref.shape
    zeros = jnp.zeros((width, width), jnp.bfloat16)
    for k, p in enumerate(range(0, pairs, 4)):
        for j, q in enumerate((p, p + 2)):
            out_ref[3 * k + j, :width, :width] = combined_ref[q]
            out_ref[3 * k + j, :width, width:] = zeros
            out_ref[3 * k + j, width:, :width] = panels_ref[q].T
            out_ref[3 * k + j, width:, width:] = panels_ref[q + 1].T
        out_ref[3 * k + 2, :width, :width] = combined_ref[p + 1]
        out_ref[3 * k + 2, :width, width:] = zeros
        out_ref[3 * k + 2, width:, :width] = zeros
        out_ref[3 * k + 2, width:, width:] = combined_ref[p + 3]


def stacked_weights(l3, combined, panels):
    pairs, width, _ = panels.shape
    return pl.pallas_call(
        weights_kernel,
        in_specs=whole(3),
        out_specs=whole(1)[0],
        out_shape=jax.ShapeDtypeStruct((pairs // 4 * 3, 2 * width, 2 * width), jnp.bfloat16),
        compiler_params=params(SMALL),
        cost_estimate=pl.CostEstimate(flops=0, bytes_accessed=panels.size * 10, transcendentals=0),
        name="stacked_weights",
    )(l3, combined, panels)


def final_kernel(flags_ref, l3_ref, normed_ref, weights_ref, r3_ref, out_ref, sems, *, block):
    triples, pairs, width, _ = l3_ref.shape
    held = triples // normed_ref.shape[0]
    stores = [pltpu.make_async_copy(out_ref.at[t], r3_ref.at[t], sems.at[t]) for t in range(triples)]

    def product(lhs, index):
        lhs = jnp.concatenate([jnp.concatenate(row, axis=1) for row in lhs], axis=0)
        return jnp.dot(lhs, weights_ref[index], preferred_element_type=jnp.float32)

    for first in range(0, triples, block):
        here = range(first, first + block)
        normed = [normed_ref[t // held, t % held * width : (t % held + 1) * width] for t in here]
        for k, p in enumerate(range(0, pairs, 4)):
            one = product([[l3_ref[t, p], normed[t - first]] for t in here], 3 * k)
            two = product([[l3_ref[t, p + 2], normed[t - first]] for t in here], 3 * k + 1)
            direct = product([[l3_ref[t, p + 1], l3_ref[t, p + 3]] for t in here], 3 * k + 2)
            sums = [
                one[:, :width],
                one[:, width:] + direct[:, :width],
                two[:, :width],
                two[:, width:] + direct[:, width:],
            ]
            for t in here:
                for j in range(4):
                    mask = flags_ref[p + j, t].astype(jnp.float32)
                    tile = sums[j][(t - first) * width : (t - first + 1) * width] * mask
                    out_ref[t, p + j] = tile.astype(jnp.bfloat16)
        for t in here:
            stores[t].start()
    for store in stores:
        store.wait()


def residual(flags, l3, normed, weights, block=2):
    triples, pairs, width, _ = l3.shape

    def kernel(*refs):
        final_kernel(*refs, block=block)

    return pl.pallas_call(
        kernel,
        in_specs=[pl.BlockSpec(memory_space=pltpu.SMEM), *whole(3)],
        out_specs=pl.BlockSpec(memory_space=pltpu.HBM),
        out_shape=jax.ShapeDtypeStruct(l3.shape, jnp.bfloat16),
        scratch_shapes=[
            pltpu.VMEM(l3.shape, jnp.bfloat16),
            pltpu.SemaphoreType.DMA((triples,)),
        ],
        compiler_params=params(MEDIUM),
        cost_estimate=pl.CostEstimate(
            flops=4 * triples * pairs * width**3, bytes_accessed=l3.size * 4, transcendentals=0
        ),
        name="residual",
    )(flags, l3, normed, weights)


def own_indices():
    me = lax.axis_index(OCC).astype(jnp.uint32)
    return [me ^ jnp.uint32(step) for step in range(lax.axis_size(OCC))]


def occ_sum(blocks, indices):
    count = blocks.shape[0]
    zero = jnp.uint32(0)
    total = None
    for step, index in enumerate(indices):
        starts = (index, *[zero] * (blocks.ndim - 1))
        block = lax.dynamic_slice(blocks, starts, (1, *blocks.shape[1:]))[0]
        if step:
            block = lax.ppermute(block, OCC, [(i, i ^ step) for i in range(count)])
        total = block if total is None else total + block
    return total


def halo(panels):
    count = lax.axis_size(VIR)
    ring = [((v, 0), ((v + 1) % count, 0)) for v in range(count)]
    ring += [((v, 1), ((v - 1) % count, 1)) for v in range(count)]
    pairs = [(2 * v + c, 2 * w + d) for (v, c), (w, d) in ring]
    mine = lax.ppermute(panels, (*VIR, "core"), pairs)
    other = lax.ppermute(mine, "core", [(0, 1), (1, 0)])
    first = lax.axis_index("core") == 0
    return jnp.where(first, mine, other), jnp.where(first, other, mine)


def shards(l3_tiles, active, panels, coupling):
    triples, pairs, width, _ = l3_tiles.shape
    vir_count, occ_count = lax.axis_size(VIR), lax.axis_size(OCC)
    near, far = lax.axis_size(NEAR), lax.axis_size("zh")
    rows = width // vir_count
    flags = active.T
    partial = partial_sums(flags, l3_tiles, panels)
    before, after = halo(panels)
    parts = lax.all_to_all(partial.reshape(near, -1, width), NEAR, 0, 0, tiled=True)

    window = jnp.concatenate([before, panels, after], axis=0)
    flat_window = window.reshape(3 * pairs, width * width).astype(jnp.float32)
    combined = jnp.dot(coupling, flat_window, precision=lax.Precision.HIGHEST)
    combined = combined.reshape(pairs, width, width).astype(jnp.bfloat16)
    parts, combined = lax.optimization_barrier((parts, combined))

    part, combined = lax.optimization_barrier((near_sums(parts), combined))
    parts = [part]
    for step in range(1, far):
        parts.append(lax.ppermute(part, "zh", [(i, i ^ step) for i in range(far)]))
    weights = stacked_weights(l3_tiles, combined, panels)
    line = lax.axis_index("zh").reshape(1)
    indices = own_indices()
    parts, weights, line, indices = lax.optimization_barrier((parts, weights, line, indices))

    copies = normed_copies(parts, line, rows, near)
    gathered = lax.all_to_all(copies, NEAR, 0, 0, tiled=True)
    high_low = gathered[:, -EXTRA:][:, : 2 * triples // near * rows].astype(jnp.float32)
    high_low = high_low.reshape(near, 2, triples // near, rows, width)
    local = (high_low[:, 0] + high_low[:, 1]).reshape(occ_count, triples // occ_count, rows, width)
    total = occ_sum(local, indices)
    r3_tiles = residual(flags, l3_tiles, gathered, weights)
    l2_block = (total / jnp.sqrt(jnp.float32(pairs * vir_count))).astype(jnp.bfloat16)
    return (r3_tiles, l2_block)


def solution(mesh):
    vir_count, occ_count = mesh.devices.shape
    split = mesh.devices.reshape(2, 4, vir_count // 16, 2, occ_count // 2, 2)
    return jax.shard_map(
        shards,
        mesh=Mesh(split, (*VIR, *OCC)),
        in_specs=(
            P(OCC, VIR, None, None),
            P(OCC, VIR),
            P(VIR, None, None),
            P(VIR, None),
        ),
        out_specs=(P(OCC, VIR, None, None), P(OCC, VIR, None)),
        check_vma=False,
    )
```

```python
import jax
import jax.numpy as jnp
from jax import lax
from jax.experimental import pallas as pl
from jax.experimental.pallas import tpu as pltpu
from jax.sharding import Mesh
from jax.sharding import PartitionSpec as P

MEDIUM = 16 * 1024 * 1024
LARGE = 60 * 1024 * 1024
SMALL = 4 * 1024 * 1024
VIR = ("yh", "x", "zh", "zl")
OCC = ("yl", "core")
NEAR = ("yh", "x", "zl")
EXTRA = 16


def params(limit):
    return pltpu.CompilerParams(vmem_limit_bytes=limit)


def whole(count):
    return [pl.BlockSpec(memory_space=pltpu.VMEM)] * count


def partial_kernel(
    flags_ref, l3_ref, panels_ref, partial_ref, flags, tiles, held, out, sems, out_sems, *, block
):
    triples, pairs, width, _ = l3_ref.shape
    half = triples // 2
    fetches = [
        pltpu.make_async_copy(flags_ref, flags, sems.at[0]),
        pltpu.make_async_copy(panels_ref, held, sems.at[1]),
    ]
    loads = [
        pltpu.make_async_copy(
            l3_ref.at[pl.ds(i * half, half)], tiles.at[pl.ds(i * half, half)], sems.at[i + 2]
        )
        for i in range(2)
    ]
    for copy in (*fetches, *loads):
        copy.start()
    for copy in fetches:
        copy.wait()
    weights = held[...].reshape(pairs * width, width)
    stores = []
    for first in range(0, triples, block):
        if first % half == 0:
            loads[first // half].wait()
        rows = []
        for t in range(first, first + block):
            masked = [
                tiles[t, p] * flags[p, t].astype(jnp.float32).astype(jnp.bfloat16)
                for p in range(pairs)
            ]
            rows.append(jnp.concatenate(masked, axis=1))
        lhs = jnp.concatenate(rows, axis=0)
        sums = jnp.dot(lhs, weights, preferred_element_type=jnp.float32)
        here = pl.ds(first * width, block * width)
        out[here] = sums.astype(jnp.bfloat16)
        store = pltpu.make_async_copy(
            out.at[here], partial_ref.at[here], out_sems.at[first // block]
        )
        store.start()
        stores.append(store)
    for store in stores:
        store.wait()


def partial_sums(flags, l3, panels, block=2):
    triples, pairs, width, _ = l3.shape

    def kernel(*refs):
        partial_kernel(*refs, block=block)

    shape = (triples * width, width)
    return pl.pallas_call(
        kernel,
        in_specs=[pl.BlockSpec(memory_space=pltpu.HBM)] * 3,
        out_specs=pl.BlockSpec(memory_space=pltpu.HBM),
        out_shape=jax.ShapeDtypeStruct(shape, jnp.bfloat16),
        scratch_shapes=[
            pltpu.SMEM(flags.shape, jnp.int32),
            pltpu.VMEM(l3.shape, jnp.bfloat16),
            pltpu.VMEM(panels.shape, jnp.bfloat16),
            pltpu.VMEM(shape, jnp.bfloat16),
            pltpu.SemaphoreType.DMA((4,)),
            pltpu.SemaphoreType.DMA((triples // block,)),
        ],
        compiler_params=params(LARGE),
        cost_estimate=pl.CostEstimate(
            flops=2 * triples * pairs * width**3, bytes_accessed=l3.size * 2, transcendentals=0
        ),
        name="partial_sums",
    )(flags, l3, panels)


def add_up(parts):
    total = parts[0][...].astype(jnp.float32)
    for part in parts[1:]:
        total = total + part[...].astype(jnp.float32)
    return total


def near_kernel(parts_ref, out_ref):
    parts = [parts_ref.at[i] for i in range(parts_ref.shape[0])]
    out_ref[...] = add_up(parts).astype(jnp.bfloat16)


def near_sums(parts):
    return pl.pallas_call(
        near_kernel,
        in_specs=whole(1),
        out_specs=whole(1)[0],
        out_shape=jax.ShapeDtypeStruct(parts.shape[1:], jnp.bfloat16),
        compiler_params=params(SMALL),
        cost_estimate=pl.CostEstimate(flops=parts.size, bytes_accessed=parts.size * 4, transcendentals=0),
        name="near_sums",
    )(parts)


def normed_kernel(line_ref, *refs, rows):
    *parts, out_ref, summed_ref = refs
    chunk, width = summed_ref.shape
    count = out_ref.shape[0]
    summed_ref[...] = add_up(parts)
    for first in range(0, chunk, width):
        tile = summed_ref[first : first + width]
        meansq = jnp.sum(tile * tile) / (width * width)
        normed = (tile * lax.rsqrt(meansq + 1e-05)).astype(jnp.bfloat16)
        for i in range(count):
            out_ref[i, first : first + width] = normed
    far = len(parts)
    for i in range(count):
        start = (i // 2 * 2 * far + line_ref[0] * 2 + i % 2) * rows
        own = [summed_ref[pl.ds(first + start, rows)] for first in range(0, chunk, width)]
        own = jnp.concatenate(own, axis=0)
        high = own.astype(jnp.bfloat16).astype(jnp.float32)
        zeros = jnp.zeros((EXTRA - 2 * own.shape[0], width), jnp.float32)
        pieces = jnp.concatenate([high, own - high, zeros], axis=0)
        out_ref[i, chunk:] = pieces.astype(jnp.bfloat16)


def normed_copies(parts, line, rows, count):
    chunk, width = parts[0].shape

    def kernel(*refs):
        normed_kernel(*refs, rows=rows)

    return pl.pallas_call(
        kernel,
        in_specs=[pl.BlockSpec(memory_space=pltpu.SMEM), *whole(len(parts))],
        out_specs=whole(1)[0],
        out_shape=jax.ShapeDtypeStruct((count, chunk + EXTRA, width), jnp.bfloat16),
        scratch_shapes=[pltpu.VMEM((chunk, width), jnp.float32)],
        compiler_params=params(SMALL),
        cost_estimate=pl.CostEstimate(
            flops=4 * chunk * width, bytes_accessed=2 * count * chunk * width, transcendentals=0
        ),
        name="normed_copies",
    )(line, *parts)


def weights_kernel(l3_ref, combined_ref, panels_ref, out_ref):
    del l3_ref
    pairs, width, _ = panels_ref.shape
    zeros = jnp.zeros((width, width), jnp.bfloat16)
    for k, p in enumerate(range(0, pairs, 4)):
        for j, q in enumerate((p, p + 2)):
            out_ref[3 * k + j, :width, :width] = combined_ref[q]
            out_ref[3 * k + j, :width, width:] = zeros
            out_ref[3 * k + j, width:, :width] = panels_ref[q].T
            out_ref[3 * k + j, width:, width:] = panels_ref[q + 1].T
        out_ref[3 * k + 2, :width, :width] = combined_ref[p + 1]
        out_ref[3 * k + 2, :width, width:] = zeros
        out_ref[3 * k + 2, width:, :width] = zeros
        out_ref[3 * k + 2, width:, width:] = combined_ref[p + 3]


def stacked_weights(l3, combined, panels):
    pairs, width, _ = panels.shape
    return pl.pallas_call(
        weights_kernel,
        in_specs=whole(3),
        out_specs=whole(1)[0],
        out_shape=jax.ShapeDtypeStruct((pairs // 4 * 3, 2 * width, 2 * width), jnp.bfloat16),
        compiler_params=params(SMALL),
        cost_estimate=pl.CostEstimate(flops=0, bytes_accessed=panels.size * 10, transcendentals=0),
        name="stacked_weights",
    )(l3, combined, panels)


def final_kernel(flags_ref, l3_ref, normed_ref, weights_ref, r3_ref, out_ref, sems, *, block):
    triples, pairs, width, _ = l3_ref.shape
    held = triples // normed_ref.shape[0]
    stores = [pltpu.make_async_copy(out_ref.at[t], r3_ref.at[t], sems.at[t]) for t in range(triples)]

    def product(lhs, index):
        lhs = jnp.concatenate([jnp.concatenate(row, axis=1) for row in lhs], axis=0)
        return jnp.dot(lhs, weights_ref[index], preferred_element_type=jnp.float32)

    for first in range(0, triples, block):
        here = range(first, first + block)
        normed = [normed_ref[t // held, t % held * width : (t % held + 1) * width] for t in here]
        for k, p in enumerate(range(0, pairs, 4)):
            one = product([[l3_ref[t, p], normed[t - first]] for t in here], 3 * k)
            two = product([[l3_ref[t, p + 2], normed[t - first]] for t in here], 3 * k + 1)
            direct = product([[l3_ref[t, p + 1], l3_ref[t, p + 3]] for t in here], 3 * k + 2)
            sums = [
                one[:, :width],
                one[:, width:] + direct[:, :width],
                two[:, :width],
                two[:, width:] + direct[:, width:],
            ]
            for t in here:
                for j in range(4):
                    mask = flags_ref[p + j, t].astype(jnp.float32)
                    tile = sums[j][(t - first) * width : (t - first + 1) * width] * mask
                    out_ref[t, p + j] = tile.astype(jnp.bfloat16)
        for t in here:
            stores[t].start()
    for store in stores:
        store.wait()


def residual(flags, l3, normed, weights, block=2):
    triples, pairs, width, _ = l3.shape

    def kernel(*refs):
        final_kernel(*refs, block=block)

    return pl.pallas_call(
        kernel,
        in_specs=[pl.BlockSpec(memory_space=pltpu.SMEM), *whole(3)],
        out_specs=pl.BlockSpec(memory_space=pltpu.HBM),
        out_shape=jax.ShapeDtypeStruct(l3.shape, jnp.bfloat16),
        scratch_shapes=[
            pltpu.VMEM(l3.shape, jnp.bfloat16),
            pltpu.SemaphoreType.DMA((triples,)),
        ],
        compiler_params=params(MEDIUM),
        cost_estimate=pl.CostEstimate(
            flops=4 * triples * pairs * width**3, bytes_accessed=l3.size * 4, transcendentals=0
        ),
        name="residual",
    )(flags, l3, normed, weights)


def own_indices():
    me = lax.axis_index(OCC).astype(jnp.uint32)
    return [me ^ jnp.uint32(step) for step in range(lax.axis_size(OCC))]


def occ_sum(blocks, indices):
    count = blocks.shape[0]
    zero = jnp.uint32(0)
    total = None
    for step in (0, 3, 1, 2):
        starts = (indices[step], *[zero] * (blocks.ndim - 1))
        block = lax.dynamic_slice(blocks, starts, (1, *blocks.shape[1:]))[0]
        if step:
            block = lax.ppermute(block, OCC, [(i, i ^ step) for i in range(count)])
        total = block if total is None else total + block
    return total


def halo(panels):
    count = lax.axis_size(VIR)
    ring = [((v, 0), ((v + 1) % count, 0)) for v in range(count)]
    ring += [((v, 1), ((v - 1) % count, 1)) for v in range(count)]
    pairs = [(2 * v + c, 2 * w + d) for (v, c), (w, d) in ring]
    mine = lax.ppermute(panels, (*VIR, "core"), pairs)
    other = lax.ppermute(mine, "core", [(0, 1), (1, 0)])
    first = lax.axis_index("core") == 0
    return jnp.where(first, mine, other), jnp.where(first, other, mine)


def shards(l3_tiles, active, panels, coupling):
    triples, pairs, width, _ = l3_tiles.shape
    vir_count, occ_count = lax.axis_size(VIR), lax.axis_size(OCC)
    near, far = lax.axis_size(NEAR), lax.axis_size("zh")
    rows = width // vir_count
    flags = active.T
    partial = partial_sums(flags, l3_tiles, panels)
    before, after = halo(panels)
    parts = lax.all_to_all(partial.reshape(near, -1, width), NEAR, 0, 0, tiled=True)

    window = jnp.concatenate([before, panels, after], axis=0)
    flat_window = window.reshape(3 * pairs, width * width).astype(jnp.float32)
    combined = jnp.dot(coupling, flat_window, precision=lax.Precision.HIGHEST)
    combined = combined.reshape(pairs, width, width).astype(jnp.bfloat16)
    parts, combined = lax.optimization_barrier((parts, combined))

    part, combined = lax.optimization_barrier((near_sums(parts), combined))
    parts = [part]
    for step in (1, 3, 2):
        parts.append(lax.ppermute(part, "zh", [(i, i ^ step) for i in range(far)]))
    weights = stacked_weights(l3_tiles, combined, panels)
    line = lax.axis_index("zh").reshape(1)
    indices = own_indices()
    parts, weights, line, indices = lax.optimization_barrier((parts, weights, line, indices))

    copies = normed_copies(parts, line, rows, near)
    gathered = lax.all_to_all(copies, NEAR, 0, 0, tiled=True)
    high_low = gathered[:, -EXTRA:][:, : 2 * triples // near * rows].astype(jnp.float32)
    high_low = high_low.reshape(near, 2, triples // near, rows, width)
    local = (high_low[:, 0] + high_low[:, 1]).reshape(occ_count, triples // occ_count, rows, width)
    total = occ_sum(local, indices)
    r3_tiles = residual(flags, l3_tiles, gathered, weights)
    l2_block = (total / jnp.sqrt(jnp.float32(pairs * vir_count))).astype(jnp.bfloat16)
    return (r3_tiles, l2_block)


def solution(mesh):
    vir_count, occ_count = mesh.devices.shape
    split = mesh.devices.reshape(2, 4, vir_count // 16, 2, occ_count // 2, 2)
    return jax.shard_map(
        shards,
        mesh=Mesh(split, (*VIR, *OCC)),
        in_specs=(
            P(OCC, VIR, None, None),
            P(OCC, VIR),
            P(VIR, None, None),
            P(VIR, None),
        ),
        out_specs=(P(OCC, VIR, None, None), P(OCC, VIR, None)),
        check_vma=False,
    )
```

```python
import jax
import jax.numpy as jnp
from jax import lax
from jax.experimental import pallas as pl
from jax.experimental.pallas import tpu as pltpu
from jax.sharding import Mesh
from jax.sharding import PartitionSpec as P

MEDIUM = 16 * 1024 * 1024
LARGE = 60 * 1024 * 1024
SMALL = 4 * 1024 * 1024
VIR = ("yh", "x", "zh", "zl")
OCC = ("yl", "core")
NEAR = ("yh", "x", "zl")
EXTRA = 16


def params(limit):
    return pltpu.CompilerParams(vmem_limit_bytes=limit)


def whole(count):
    return [pl.BlockSpec(memory_space=pltpu.VMEM)] * count


def partial_kernel(
    flags_ref, l3_ref, panels_ref, partial_ref, flags, tiles, held, out, sems, out_sems, *, block
):
    triples, pairs, width, _ = l3_ref.shape
    half = triples // 2
    fetches = [
        pltpu.make_async_copy(flags_ref, flags, sems.at[0]),
        pltpu.make_async_copy(panels_ref, held, sems.at[1]),
    ]
    loads = [
        pltpu.make_async_copy(
            l3_ref.at[pl.ds(i * half, half)], tiles.at[pl.ds(i * half, half)], sems.at[i + 2]
        )
        for i in range(2)
    ]
    for copy in (*fetches, *loads):
        copy.start()
    for copy in fetches:
        copy.wait()
    weights = held[...].reshape(pairs * width, width)
    stores = []
    for first in range(0, triples, block):
        if first % half == 0:
            loads[first // half].wait()
        rows = []
        for t in range(first, first + block):
            masked = [
                tiles[t, p] * flags[p, t].astype(jnp.float32).astype(jnp.bfloat16)
                for p in range(pairs)
            ]
            rows.append(jnp.concatenate(masked, axis=1))
        lhs = jnp.concatenate(rows, axis=0)
        sums = jnp.dot(lhs, weights, preferred_element_type=jnp.float32)
        here = pl.ds(first * width, block * width)
        out[here] = sums.astype(jnp.bfloat16)
        store = pltpu.make_async_copy(
            out.at[here], partial_ref.at[here], out_sems.at[first // block]
        )
        store.start()
        stores.append(store)
    for store in stores:
        store.wait()


def partial_sums(flags, l3, panels, block=2):
    triples, pairs, width, _ = l3.shape

    def kernel(*refs):
        partial_kernel(*refs, block=block)

    shape = (triples * width, width)
    return pl.pallas_call(
        kernel,
        in_specs=[pl.BlockSpec(memory_space=pltpu.HBM)] * 3,
        out_specs=pl.BlockSpec(memory_space=pltpu.HBM),
        out_shape=jax.ShapeDtypeStruct(shape, jnp.bfloat16),
        scratch_shapes=[
            pltpu.SMEM(flags.shape, jnp.int32),
            pltpu.VMEM(l3.shape, jnp.bfloat16),
            pltpu.VMEM(panels.shape, jnp.bfloat16),
            pltpu.VMEM(shape, jnp.bfloat16),
            pltpu.SemaphoreType.DMA((4,)),
            pltpu.SemaphoreType.DMA((triples // block,)),
        ],
        compiler_params=params(LARGE),
        cost_estimate=pl.CostEstimate(
            flops=2 * triples * pairs * width**3, bytes_accessed=l3.size * 2, transcendentals=0
        ),
        name="partial_sums",
    )(flags, l3, panels)


def add_up(parts):
    total = parts[0][...].astype(jnp.float32)
    for part in parts[1:]:
        total = total + part[...].astype(jnp.float32)
    return total


def near_kernel(parts_ref, out_ref):
    parts = [parts_ref.at[i] for i in range(parts_ref.shape[0])]
    out_ref[...] = add_up(parts).astype(jnp.bfloat16)


def near_sums(parts):
    return pl.pallas_call(
        near_kernel,
        in_specs=whole(1),
        out_specs=whole(1)[0],
        out_shape=jax.ShapeDtypeStruct(parts.shape[1:], jnp.bfloat16),
        compiler_params=params(SMALL),
        cost_estimate=pl.CostEstimate(flops=parts.size, bytes_accessed=parts.size * 4, transcendentals=0),
        name="near_sums",
    )(parts)


def normed_kernel(line_ref, *refs, rows):
    *parts, out_ref, summed_ref = refs
    chunk, width = summed_ref.shape
    count = out_ref.shape[0]
    summed_ref[...] = add_up(parts)
    for first in range(0, chunk, width):
        tile = summed_ref[first : first + width]
        meansq = jnp.sum(tile * tile) / (width * width)
        normed = (tile * lax.rsqrt(meansq + 1e-05)).astype(jnp.bfloat16)
        for i in range(count):
            out_ref[i, first : first + width] = normed
    far = len(parts)
    for i in range(count):
        start = (i // 2 * 2 * far + line_ref[0] * 2 + i % 2) * rows
        own = [summed_ref[pl.ds(first + start, rows)] for first in range(0, chunk, width)]
        own = jnp.concatenate(own, axis=0)
        high = own.astype(jnp.bfloat16).astype(jnp.float32)
        zeros = jnp.zeros((EXTRA - 2 * own.shape[0], width), jnp.float32)
        pieces = jnp.concatenate([high, own - high, zeros], axis=0)
        out_ref[i, chunk:] = pieces.astype(jnp.bfloat16)


def normed_copies(parts, line, rows, count):
    chunk, width = parts[0].shape

    def kernel(*refs):
        normed_kernel(*refs, rows=rows)

    return pl.pallas_call(
        kernel,
        in_specs=[pl.BlockSpec(memory_space=pltpu.SMEM), *whole(len(parts))],
        out_specs=whole(1)[0],
        out_shape=jax.ShapeDtypeStruct((count, chunk + EXTRA, width), jnp.bfloat16),
        scratch_shapes=[pltpu.VMEM((chunk, width), jnp.float32)],
        compiler_params=params(SMALL),
        cost_estimate=pl.CostEstimate(
            flops=4 * chunk * width, bytes_accessed=2 * count * chunk * width, transcendentals=0
        ),
        name="normed_copies",
    )(line, *parts)


def weights_kernel(l3_ref, combined_ref, panels_ref, out_ref):
    del l3_ref
    pairs, width, _ = panels_ref.shape
    zeros = jnp.zeros((width, width), jnp.bfloat16)
    for k, p in enumerate(range(0, pairs, 4)):
        for j, q in enumerate((p, p + 2)):
            out_ref[3 * k + j, :width, :width] = combined_ref[q]
            out_ref[3 * k + j, :width, width:] = zeros
            out_ref[3 * k + j, width:, :width] = panels_ref[q].T
            out_ref[3 * k + j, width:, width:] = panels_ref[q + 1].T
        out_ref[3 * k + 2, :width, :width] = combined_ref[p + 1]
        out_ref[3 * k + 2, :width, width:] = zeros
        out_ref[3 * k + 2, width:, :width] = zeros
        out_ref[3 * k + 2, width:, width:] = combined_ref[p + 3]


def stacked_weights(l3, combined, panels):
    pairs, width, _ = panels.shape
    return pl.pallas_call(
        weights_kernel,
        in_specs=whole(3),
        out_specs=whole(1)[0],
        out_shape=jax.ShapeDtypeStruct((pairs // 4 * 3, 2 * width, 2 * width), jnp.bfloat16),
        compiler_params=params(SMALL),
        cost_estimate=pl.CostEstimate(flops=0, bytes_accessed=panels.size * 10, transcendentals=0),
        name="stacked_weights",
    )(l3, combined, panels)


def final_kernel(
    core_ref, flags_ref, l3_ref, normed_ref, weights_ref, r3_ref, out_ref, flags, sem, sems, *, block
):
    triples, pairs, width, _ = l3_ref.shape
    held = triples // normed_ref.shape[0]
    fetch = pltpu.make_async_copy(flags_ref, flags, sem)
    fetch.start()
    stores = [pltpu.make_async_copy(out_ref.at[t], r3_ref.at[t], sems.at[t]) for t in range(triples)]

    def product(lhs, index):
        lhs = jnp.concatenate([jnp.concatenate(row, axis=1) for row in lhs], axis=0)
        return jnp.dot(lhs, weights_ref[index], preferred_element_type=jnp.float32)

    fetch.wait()
    for first in range(0, triples, block):
        here = range(first, first + block)
        normed = [normed_ref[t // held, t % held * width : (t % held + 1) * width] for t in here]
        for k, p in enumerate(range(0, pairs, 4)):
            one = product([[l3_ref[t, p], normed[t - first]] for t in here], 3 * k)
            two = product([[l3_ref[t, p + 2], normed[t - first]] for t in here], 3 * k + 1)
            direct = product([[l3_ref[t, p + 1], l3_ref[t, p + 3]] for t in here], 3 * k + 2)
            sums = [
                one[:, :width],
                one[:, width:] + direct[:, :width],
                two[:, :width],
                two[:, width:] + direct[:, width:],
            ]
            for t in here:
                for j in range(4):
                    mask = flags[p + j, t].astype(jnp.float32)
                    tile = sums[j][(t - first) * width : (t - first + 1) * width] * mask
                    out_ref[t, p + j] = tile.astype(jnp.bfloat16)
        for t in here:
            stores[t].start()
    for store in stores:
        store.wait()


def residual(turn, core, flags, l3, normed, weights, before=None, block=2):
    triples, pairs, width, _ = l3.shape

    def kernel(core_ref, *refs):
        refs = refs[:4] + refs[5:] if before is not None else refs

        @pl.when(core_ref[0] == turn)
        def _():
            final_kernel(core_ref, *refs, block=block)

    hbm = pl.BlockSpec(memory_space=pltpu.HBM)
    operands = [core, flags, l3, normed, weights]
    in_specs = [pl.BlockSpec(memory_space=pltpu.SMEM), hbm, *whole(3)]
    if before is not None:
        operands.append(before)
        in_specs.append(hbm)
    return pl.pallas_call(
        kernel,
        in_specs=in_specs,
        out_specs=hbm,
        out_shape=jax.ShapeDtypeStruct(l3.shape, jnp.bfloat16),
        input_output_aliases={} if before is None else {5: 0},
        scratch_shapes=[
            pltpu.VMEM(l3.shape, jnp.bfloat16),
            pltpu.SMEM(flags.shape, jnp.int32),
            pltpu.SemaphoreType.DMA,
            pltpu.SemaphoreType.DMA((triples,)),
        ],
        compiler_params=params(MEDIUM),
        cost_estimate=pl.CostEstimate(
            flops=4 * triples * pairs * width**3, bytes_accessed=l3.size * 4, transcendentals=0
        ),
        name="residual",
    )(*operands)


def own_indices():
    me = lax.axis_index(OCC).astype(jnp.uint32)
    return [me ^ jnp.uint32(step) for step in range(lax.axis_size(OCC))]


def occ_sum(blocks, indices):
    count = blocks.shape[0]
    zero = jnp.uint32(0)
    total = None
    for step in (0, 3, 2, 1):
        starts = (indices[step], *[zero] * (blocks.ndim - 1))
        block = lax.dynamic_slice(blocks, starts, (1, *blocks.shape[1:]))[0]
        if step:
            block = lax.ppermute(block, OCC, [(i, i ^ step) for i in range(count)])
        total = block if total is None else total + block
    return total


def halo(panels):
    count = lax.axis_size(VIR)
    ring = [((v, 0), ((v + 1) % count, 0)) for v in range(count)]
    ring += [((v, 1), ((v - 1) % count, 1)) for v in range(count)]
    pairs = [(2 * v + c, 2 * w + d) for (v, c), (w, d) in ring]
    mine = lax.ppermute(panels, (*VIR, "core"), pairs)
    other = lax.ppermute(mine, "core", [(0, 1), (1, 0)])
    first = lax.axis_index("core") == 0
    return jnp.where(first, mine, other), jnp.where(first, other, mine)


def shards(l3_tiles, active, panels, coupling):
    triples, pairs, width, _ = l3_tiles.shape
    vir_count, occ_count = lax.axis_size(VIR), lax.axis_size(OCC)
    near, far = lax.axis_size(NEAR), lax.axis_size("zh")
    rows = width // vir_count
    flags = active.T
    partial = partial_sums(flags, l3_tiles, panels)
    before, after = halo(panels)
    parts = lax.all_to_all(partial.reshape(near, -1, width), NEAR, 0, 0, tiled=True)

    window = jnp.concatenate([before, panels, after], axis=0)
    flat_window = window.reshape(3 * pairs, width * width).astype(jnp.float32)
    combined = jnp.dot(coupling, flat_window, precision=lax.Precision.HIGHEST)
    combined = combined.reshape(pairs, width, width).astype(jnp.bfloat16)
    parts, combined = lax.optimization_barrier((parts, combined))

    part, combined = lax.optimization_barrier((near_sums(parts), combined))
    parts = [part]
    for step in (2, 3, 1):
        parts.append(lax.ppermute(part, "zh", [(i, i ^ step) for i in range(far)]))
    weights = stacked_weights(l3_tiles, combined, panels)
    line = lax.axis_index("zh").reshape(1)
    core = lax.axis_index("core").reshape(1)
    indices = own_indices()
    parts, weights, line, core, indices = lax.optimization_barrier(
        (parts, weights, line, core, indices)
    )

    copies = normed_copies(parts, line, rows, near)
    gathered = lax.all_to_all(copies, NEAR, 0, 0, tiled=True)
    high_low = gathered[:, -EXTRA:][:, : 2 * triples // near * rows].astype(jnp.float32)
    high_low = high_low.reshape(near, 2, triples // near, rows, width)
    local = (high_low[:, 0] + high_low[:, 1]).reshape(occ_count, triples // occ_count, rows, width)
    r3_tiles = residual(1, core, flags, l3_tiles, gathered, weights)
    local, r3_tiles = lax.optimization_barrier((local, r3_tiles))
    total = occ_sum(local, indices)
    r3_tiles = residual(0, core, flags, l3_tiles, gathered, weights, r3_tiles)
    l2_block = (total / jnp.sqrt(jnp.float32(pairs * vir_count))).astype(jnp.bfloat16)
    return (r3_tiles, l2_block)


def solution(mesh):
    vir_count, occ_count = mesh.devices.shape
    split = mesh.devices.reshape(2, 4, vir_count // 16, 2, occ_count // 2, 2)
    return jax.shard_map(
        shards,
        mesh=Mesh(split, (*VIR, *OCC)),
        in_specs=(
            P(OCC, VIR, None, None),
            P(OCC, VIR),
            P(VIR, None, None),
            P(VIR, None),
        ),
        out_specs=(P(OCC, VIR, None, None), P(OCC, VIR, None)),
        check_vma=False,
    )
```

```python
import jax
import jax.numpy as jnp
from jax import lax
from jax.experimental import pallas as pl
from jax.experimental.pallas import tpu as pltpu
from jax.sharding import Mesh
from jax.sharding import PartitionSpec as P

MEDIUM = 16 * 1024 * 1024
LARGE = 60 * 1024 * 1024
SMALL = 4 * 1024 * 1024
VIR = ("yh", "x", "zh", "zl")
OCC = ("yl", "core")
NEAR = ("yh", "x", "zl")
EXTRA = 16


def params(limit):
    return pltpu.CompilerParams(vmem_limit_bytes=limit)


def whole(count):
    return [pl.BlockSpec(memory_space=pltpu.VMEM)] * count


def partial_kernel(
    flags_ref, l3_ref, panels_ref, partial_ref, flags, tiles, held, out, sems, out_sems, *, block
):
    triples, pairs, width, _ = l3_ref.shape
    half = triples // 2
    fetches = [
        pltpu.make_async_copy(flags_ref, flags, sems.at[0]),
        pltpu.make_async_copy(panels_ref, held, sems.at[1]),
    ]
    loads = [
        pltpu.make_async_copy(
            l3_ref.at[pl.ds(i * half, half)], tiles.at[pl.ds(i * half, half)], sems.at[i + 2]
        )
        for i in range(2)
    ]
    for copy in (*fetches, *loads):
        copy.start()
    for copy in fetches:
        copy.wait()
    weights = held[...].reshape(pairs * width, width)
    stores = []
    for first in range(0, triples, block):
        if first % half == 0:
            loads[first // half].wait()
        rows = []
        for t in range(first, first + block):
            masked = [
                tiles[t, p] * flags[p, t].astype(jnp.float32).astype(jnp.bfloat16)
                for p in range(pairs)
            ]
            rows.append(jnp.concatenate(masked, axis=1))
        lhs = jnp.concatenate(rows, axis=0)
        sums = jnp.dot(lhs, weights, preferred_element_type=jnp.float32)
        here = pl.ds(first * width, block * width)
        out[here] = sums.astype(jnp.bfloat16)
        store = pltpu.make_async_copy(
            out.at[here], partial_ref.at[here], out_sems.at[first // block]
        )
        store.start()
        stores.append(store)
    for store in stores:
        store.wait()


def partial_sums(flags, l3, panels, block=2):
    triples, pairs, width, _ = l3.shape

    def kernel(*refs):
        partial_kernel(*refs, block=block)

    shape = (triples * width, width)
    return pl.pallas_call(
        kernel,
        in_specs=[pl.BlockSpec(memory_space=pltpu.HBM)] * 3,
        out_specs=pl.BlockSpec(memory_space=pltpu.HBM),
        out_shape=jax.ShapeDtypeStruct(shape, jnp.bfloat16),
        scratch_shapes=[
            pltpu.SMEM(flags.shape, jnp.int32),
            pltpu.VMEM(l3.shape, jnp.bfloat16),
            pltpu.VMEM(panels.shape, jnp.bfloat16),
            pltpu.VMEM(shape, jnp.bfloat16),
            pltpu.SemaphoreType.DMA((4,)),
            pltpu.SemaphoreType.DMA((triples // block,)),
        ],
        compiler_params=params(LARGE),
        cost_estimate=pl.CostEstimate(
            flops=2 * triples * pairs * width**3, bytes_accessed=l3.size * 2, transcendentals=0
        ),
        name="partial_sums",
    )(flags, l3, panels)


def add_up(parts):
    total = parts[0][...].astype(jnp.float32)
    for part in parts[1:]:
        total = total + part[...].astype(jnp.float32)
    return total


def near_kernel(parts_ref, out_ref):
    parts = [parts_ref.at[i] for i in range(parts_ref.shape[0])]
    out_ref[...] = add_up(parts).astype(jnp.bfloat16)


def near_sums(parts):
    return pl.pallas_call(
        near_kernel,
        in_specs=whole(1),
        out_specs=whole(1)[0],
        out_shape=jax.ShapeDtypeStruct(parts.shape[1:], jnp.bfloat16),
        compiler_params=params(SMALL),
        cost_estimate=pl.CostEstimate(flops=parts.size, bytes_accessed=parts.size * 4, transcendentals=0),
        name="near_sums",
    )(parts)


def normed_kernel(line_ref, *refs, rows):
    *parts, out_ref, summed_ref = refs
    chunk, width = summed_ref.shape
    count = out_ref.shape[0]
    summed_ref[...] = add_up(parts)
    for first in range(0, chunk, width):
        tile = summed_ref[first : first + width]
        meansq = jnp.sum(tile * tile) / (width * width)
        normed = (tile * lax.rsqrt(meansq + 1e-05)).astype(jnp.bfloat16)
        for i in range(count):
            out_ref[i, first : first + width] = normed
    far = len(parts)
    for i in range(count):
        start = (i // 2 * 2 * far + line_ref[0] * 2 + i % 2) * rows
        own = [summed_ref[pl.ds(first + start, rows)] for first in range(0, chunk, width)]
        own = jnp.concatenate(own, axis=0)
        high = own.astype(jnp.bfloat16).astype(jnp.float32)
        zeros = jnp.zeros((EXTRA - 2 * own.shape[0], width), jnp.float32)
        pieces = jnp.concatenate([high, own - high, zeros], axis=0)
        out_ref[i, chunk:] = pieces.astype(jnp.bfloat16)


def normed_copies(parts, line, rows, count):
    chunk, width = parts[0].shape

    def kernel(*refs):
        normed_kernel(*refs, rows=rows)

    return pl.pallas_call(
        kernel,
        in_specs=[pl.BlockSpec(memory_space=pltpu.SMEM), *whole(len(parts))],
        out_specs=whole(1)[0],
        out_shape=jax.ShapeDtypeStruct((count, chunk + EXTRA, width), jnp.bfloat16),
        scratch_shapes=[pltpu.VMEM((chunk, width), jnp.float32)],
        compiler_params=params(SMALL),
        cost_estimate=pl.CostEstimate(
            flops=4 * chunk * width, bytes_accessed=2 * count * chunk * width, transcendentals=0
        ),
        name="normed_copies",
    )(line, *parts)


def weights_kernel(l3_ref, combined_ref, panels_ref, out_ref):
    del l3_ref
    pairs, width, _ = panels_ref.shape
    zeros = jnp.zeros((width, width), jnp.bfloat16)
    for k, p in enumerate(range(0, pairs, 4)):
        for j, q in enumerate((p, p + 2)):
            out_ref[3 * k + j, :width, :width] = combined_ref[q]
            out_ref[3 * k + j, :width, width:] = zeros
            out_ref[3 * k + j, width:, :width] = panels_ref[q].T
            out_ref[3 * k + j, width:, width:] = panels_ref[q + 1].T
        out_ref[3 * k + 2, :width, :width] = combined_ref[p + 1]
        out_ref[3 * k + 2, :width, width:] = zeros
        out_ref[3 * k + 2, width:, :width] = zeros
        out_ref[3 * k + 2, width:, width:] = combined_ref[p + 3]


def stacked_weights(l3, combined, panels):
    pairs, width, _ = panels.shape
    return pl.pallas_call(
        weights_kernel,
        in_specs=whole(3),
        out_specs=whole(1)[0],
        out_shape=jax.ShapeDtypeStruct((pairs // 4 * 3, 2 * width, 2 * width), jnp.bfloat16),
        compiler_params=params(SMALL),
        cost_estimate=pl.CostEstimate(flops=0, bytes_accessed=panels.size * 10, transcendentals=0),
        name="stacked_weights",
    )(l3, combined, panels)


def final_kernel(
    core_ref, flags_ref, l3_ref, normed_ref, weights_ref, r3_ref, out_ref, flags, sem, sems, *, block
):
    triples, pairs, width, _ = l3_ref.shape
    held = triples // normed_ref.shape[0]
    fetch = pltpu.make_async_copy(flags_ref, flags, sem)
    fetch.start()
    stores = [pltpu.make_async_copy(out_ref.at[t], r3_ref.at[t], sems.at[t]) for t in range(triples)]

    def product(lhs, index):
        lhs = jnp.concatenate([jnp.concatenate(row, axis=1) for row in lhs], axis=0)
        return jnp.dot(lhs, weights_ref[index], preferred_element_type=jnp.float32)

    edges = [0, 1, *range(2, triples - 1, block), triples - 1, triples]
    for first, after in zip(edges, edges[1:]):
        here = range(first, after)
        normed = [normed_ref[t // held, t % held * width : (t % held + 1) * width] for t in here]
        for k, p in enumerate(range(0, pairs, 4)):
            one = product([[l3_ref[t, p], normed[t - first]] for t in here], 3 * k)
            two = product([[l3_ref[t, p + 2], normed[t - first]] for t in here], 3 * k + 1)
            direct = product([[l3_ref[t, p + 1], l3_ref[t, p + 3]] for t in here], 3 * k + 2)
            if first == 0 and k == 0:
                fetch.wait()
            sums = [
                one[:, :width],
                one[:, width:] + direct[:, :width],
                two[:, :width],
                two[:, width:] + direct[:, width:],
            ]
            for t in here:
                for j in range(4):
                    mask = flags[p + j, t].astype(jnp.float32)
                    tile = sums[j][(t - first) * width : (t - first + 1) * width] * mask
                    out_ref[t, p + j] = tile.astype(jnp.bfloat16)
        for t in here:
            stores[t].start()
    for store in stores:
        store.wait()


def residual(turn, core, flags, l3, normed, weights, before=None, block=2):
    triples, pairs, width, _ = l3.shape

    def kernel(core_ref, *refs):
        refs = refs[:4] + refs[5:] if before is not None else refs

        @pl.when(core_ref[0] == turn)
        def _():
            final_kernel(core_ref, *refs, block=block)

    hbm = pl.BlockSpec(memory_space=pltpu.HBM)
    operands = [core, flags, l3, normed, weights]
    in_specs = [pl.BlockSpec(memory_space=pltpu.SMEM), hbm, *whole(3)]
    if before is not None:
        operands.append(before)
        in_specs.append(hbm)
    return pl.pallas_call(
        kernel,
        in_specs=in_specs,
        out_specs=hbm,
        out_shape=jax.ShapeDtypeStruct(l3.shape, jnp.bfloat16),
        input_output_aliases={} if before is None else {5: 0},
        scratch_shapes=[
            pltpu.VMEM(l3.shape, jnp.bfloat16),
            pltpu.SMEM(flags.shape, jnp.int32),
            pltpu.SemaphoreType.DMA,
            pltpu.SemaphoreType.DMA((triples,)),
        ],
        compiler_params=params(MEDIUM),
        cost_estimate=pl.CostEstimate(
            flops=4 * triples * pairs * width**3, bytes_accessed=l3.size * 4, transcendentals=0
        ),
        name="residual",
    )(*operands)


def own_indices():
    me = lax.axis_index(OCC).astype(jnp.uint32)
    return [me ^ jnp.uint32(step) for step in range(lax.axis_size(OCC))]


def occ_sum(blocks, indices):
    count = blocks.shape[0]
    zero = jnp.uint32(0)
    total = None
    for step in (0, 2, 3, 1):
        starts = (indices[step], *[zero] * (blocks.ndim - 1))
        block = lax.dynamic_slice(blocks, starts, (1, *blocks.shape[1:]))[0]
        if step:
            block = lax.ppermute(block, OCC, [(i, i ^ step) for i in range(count)])
        total = block if total is None else total + block
    return total


def halo(panels):
    count = lax.axis_size(VIR)
    ring = [((v, 0), ((v + 1) % count, 0)) for v in range(count)]
    ring += [((v, 1), ((v - 1) % count, 1)) for v in range(count)]
    pairs = [(2 * v + c, 2 * w + d) for (v, c), (w, d) in ring]
    mine = lax.ppermute(panels, (*VIR, "core"), pairs)
    other = lax.ppermute(mine, "core", [(0, 1), (1, 0)])
    first = lax.axis_index("core") == 0
    return jnp.where(first, mine, other), jnp.where(first, other, mine)


def shards(l3_tiles, active, panels, coupling):
    triples, pairs, width, _ = l3_tiles.shape
    vir_count, occ_count = lax.axis_size(VIR), lax.axis_size(OCC)
    near, far = lax.axis_size(NEAR), lax.axis_size("zh")
    rows = width // vir_count
    flags = active.T
    partial = partial_sums(flags, l3_tiles, panels)
    before, after = halo(panels)
    parts = lax.all_to_all(partial.reshape(near, -1, width), NEAR, 0, 0, tiled=True)

    window = jnp.concatenate([before, panels, after], axis=0)
    flat_window = window.reshape(3 * pairs, width * width).astype(jnp.float32)
    combined = jnp.dot(coupling, flat_window, precision=lax.Precision.HIGHEST)
    combined = combined.reshape(pairs, width, width).astype(jnp.bfloat16)
    parts, combined = lax.optimization_barrier((parts, combined))

    part, combined = lax.optimization_barrier((near_sums(parts), combined))
    parts = [part]
    for step in (2, 3, 1):
        parts.append(lax.ppermute(part, "zh", [(i, i ^ step) for i in range(far)]))
    weights = stacked_weights(l3_tiles, combined, panels)
    line = lax.axis_index("zh").reshape(1)
    core = lax.axis_index("core").reshape(1)
    indices = own_indices()
    parts, weights, line, core, indices = lax.optimization_barrier(
        (parts, weights, line, core, indices)
    )

    copies = normed_copies(parts, line, rows, near)
    gathered = lax.all_to_all(copies, NEAR, 0, 0, tiled=True)
    high_low = gathered[:, -EXTRA:][:, : 2 * triples // near * rows].astype(jnp.float32)
    high_low = high_low.reshape(near, 2, triples // near, rows, width)
    local = (high_low[:, 0] + high_low[:, 1]).reshape(occ_count, triples // occ_count, rows, width)
    r3_tiles = residual(1, core, flags, l3_tiles, gathered, weights)
    local, r3_tiles = lax.optimization_barrier((local, r3_tiles))
    total = occ_sum(local, indices)
    r3_tiles = residual(0, core, flags, l3_tiles, gathered, weights, r3_tiles)
    l2_block = (total / jnp.sqrt(jnp.float32(pairs * vir_count))).astype(jnp.bfloat16)
    return (r3_tiles, l2_block)


def solution(mesh):
    vir_count, occ_count = mesh.devices.shape
    split = mesh.devices.reshape(2, 4, vir_count // 16, 2, occ_count // 2, 2)
    return jax.shard_map(
        shards,
        mesh=Mesh(split, (*VIR, *OCC)),
        in_specs=(
            P(OCC, VIR, None, None),
            P(OCC, VIR),
            P(VIR, None, None),
            P(VIR, None),
        ),
        out_specs=(P(OCC, VIR, None, None), P(OCC, VIR, None)),
        check_vma=False,
    )
```

```python
import jax
import jax.numpy as jnp
from jax import lax
from jax.experimental import pallas as pl
from jax.experimental.pallas import tpu as pltpu
from jax.sharding import Mesh
from jax.sharding import PartitionSpec as P

MEDIUM = 16 * 1024 * 1024
LARGE = 60 * 1024 * 1024
SMALL = 4 * 1024 * 1024
VIR = ("yh", "x", "zh", "zl")
OCC = ("yl", "core")
NEAR = ("yh", "x", "zl")
EXTRA = 16


def params(limit):
    return pltpu.CompilerParams(vmem_limit_bytes=limit)


def whole(count):
    return [pl.BlockSpec(memory_space=pltpu.VMEM)] * count


def partial_kernel(
    flags_ref, l3_ref, panels_ref, partial_ref, flags, tiles, held, out, sems, out_sems, *, block
):
    triples, pairs, width, _ = l3_ref.shape
    half = triples // 2
    fetches = [
        pltpu.make_async_copy(flags_ref, flags, sems.at[0]),
        pltpu.make_async_copy(panels_ref, held, sems.at[1]),
    ]
    loads = [
        pltpu.make_async_copy(
            l3_ref.at[pl.ds(i * half, half)], tiles.at[pl.ds(i * half, half)], sems.at[i + 2]
        )
        for i in range(2)
    ]
    for copy in (*fetches, *loads):
        copy.start()
    for copy in fetches:
        copy.wait()
    weights = held[...].reshape(pairs * width, width)
    stores = []
    for first in range(0, triples, block):
        if first % half == 0:
            loads[first // half].wait()
        rows = []
        for t in range(first, first + block):
            masked = [
                tiles[t, p] * flags[p, t].astype(jnp.float32).astype(jnp.bfloat16)
                for p in range(pairs)
            ]
            rows.append(jnp.concatenate(masked, axis=1))
        lhs = jnp.concatenate(rows, axis=0)
        sums = jnp.dot(lhs, weights, preferred_element_type=jnp.float32)
        here = pl.ds(first * width, block * width)
        out[here] = sums.astype(jnp.bfloat16)
        store = pltpu.make_async_copy(
            out.at[here], partial_ref.at[here], out_sems.at[first // block]
        )
        store.start()
        stores.append(store)
    for store in stores:
        store.wait()


def partial_sums(flags, l3, panels, block=2):
    triples, pairs, width, _ = l3.shape

    def kernel(*refs):
        partial_kernel(*refs, block=block)

    shape = (triples * width, width)
    return pl.pallas_call(
        kernel,
        in_specs=[pl.BlockSpec(memory_space=pltpu.HBM)] * 3,
        out_specs=pl.BlockSpec(memory_space=pltpu.HBM),
        out_shape=jax.ShapeDtypeStruct(shape, jnp.bfloat16),
        scratch_shapes=[
            pltpu.SMEM(flags.shape, jnp.int32),
            pltpu.VMEM(l3.shape, jnp.bfloat16),
            pltpu.VMEM(panels.shape, jnp.bfloat16),
            pltpu.VMEM(shape, jnp.bfloat16),
            pltpu.SemaphoreType.DMA((4,)),
            pltpu.SemaphoreType.DMA((triples // block,)),
        ],
        compiler_params=params(LARGE),
        cost_estimate=pl.CostEstimate(
            flops=2 * triples * pairs * width**3, bytes_accessed=l3.size * 2, transcendentals=0
        ),
        name="partial_sums",
    )(flags, l3, panels)


def add_up(parts):
    total = parts[0][...].astype(jnp.float32)
    for part in parts[1:]:
        total = total + part[...].astype(jnp.float32)
    return total


def near_kernel(parts_ref, out_ref):
    parts = [parts_ref.at[i] for i in range(parts_ref.shape[0])]
    out_ref[...] = add_up(parts).astype(jnp.bfloat16)


def near_sums(parts):
    return pl.pallas_call(
        near_kernel,
        in_specs=whole(1),
        out_specs=whole(1)[0],
        out_shape=jax.ShapeDtypeStruct(parts.shape[1:], jnp.bfloat16),
        compiler_params=params(SMALL),
        cost_estimate=pl.CostEstimate(flops=parts.size, bytes_accessed=parts.size * 4, transcendentals=0),
        name="near_sums",
    )(parts)


def normed_kernel(line_ref, *refs, rows):
    *parts, out_ref, summed_ref = refs
    chunk, width = summed_ref.shape
    count = out_ref.shape[0]
    summed_ref[...] = add_up(parts)
    for first in range(0, chunk, width):
        tile = summed_ref[first : first + width]
        meansq = jnp.sum(tile * tile) / (width * width)
        normed = (tile * lax.rsqrt(meansq + 1e-05)).astype(jnp.bfloat16)
        for i in range(count):
            out_ref[i, first : first + width] = normed
    far = len(parts)
    for i in range(count):
        start = (i // 2 * 2 * far + line_ref[0] * 2 + i % 2) * rows
        own = [summed_ref[pl.ds(first + start, rows)] for first in range(0, chunk, width)]
        own = jnp.concatenate(own, axis=0)
        high = own.astype(jnp.bfloat16).astype(jnp.float32)
        zeros = jnp.zeros((EXTRA - 2 * own.shape[0], width), jnp.float32)
        pieces = jnp.concatenate([high, own - high, zeros], axis=0)
        out_ref[i, chunk:] = pieces.astype(jnp.bfloat16)


def normed_copies(parts, line, rows, count):
    chunk, width = parts[0].shape

    def kernel(*refs):
        normed_kernel(*refs, rows=rows)

    return pl.pallas_call(
        kernel,
        in_specs=[pl.BlockSpec(memory_space=pltpu.SMEM), *whole(len(parts))],
        out_specs=whole(1)[0],
        out_shape=jax.ShapeDtypeStruct((count, chunk + EXTRA, width), jnp.bfloat16),
        scratch_shapes=[pltpu.VMEM((chunk, width), jnp.float32)],
        compiler_params=params(SMALL),
        cost_estimate=pl.CostEstimate(
            flops=4 * chunk * width, bytes_accessed=2 * count * chunk * width, transcendentals=0
        ),
        name="normed_copies",
    )(line, *parts)


def weights_kernel(l3_ref, combined_ref, panels_ref, out_ref):
    del l3_ref
    pairs, width, _ = panels_ref.shape
    zeros = jnp.zeros((width, width), jnp.bfloat16)
    for k, p in enumerate(range(0, pairs, 4)):
        for j, q in enumerate((p, p + 2)):
            out_ref[3 * k + j, :width, :width] = combined_ref[q]
            out_ref[3 * k + j, :width, width:] = zeros
            out_ref[3 * k + j, width:, :width] = panels_ref[q].T
            out_ref[3 * k + j, width:, width:] = panels_ref[q + 1].T
        out_ref[3 * k + 2, :width, :width] = combined_ref[p + 1]
        out_ref[3 * k + 2, :width, width:] = zeros
        out_ref[3 * k + 2, width:, :width] = zeros
        out_ref[3 * k + 2, width:, width:] = combined_ref[p + 3]


def stacked_weights(l3, combined, panels):
    pairs, width, _ = panels.shape
    return pl.pallas_call(
        weights_kernel,
        in_specs=whole(3),
        out_specs=whole(1)[0],
        out_shape=jax.ShapeDtypeStruct((pairs // 4 * 3, 2 * width, 2 * width), jnp.bfloat16),
        compiler_params=params(SMALL),
        cost_estimate=pl.CostEstimate(flops=0, bytes_accessed=panels.size * 10, transcendentals=0),
        name="stacked_weights",
    )(l3, combined, panels)


def final_kernel(
    core_ref, flags_ref, l3_ref, normed_ref, weights_ref, r3_ref, out_ref, flags, sem, sems, *, block
):
    triples, pairs, width, _ = l3_ref.shape
    held = triples // normed_ref.shape[0]
    fetch = pltpu.make_async_copy(flags_ref, flags, sem)
    fetch.start()
    stores = [pltpu.make_async_copy(out_ref.at[t], r3_ref.at[t], sems.at[t]) for t in range(triples)]

    def product(lhs, index):
        lhs = jnp.concatenate([jnp.concatenate(row, axis=1) for row in lhs], axis=0)
        return jnp.dot(lhs, weights_ref[index], preferred_element_type=jnp.float32)

    edges = [0, 1, *range(2, triples - 1, block), triples - 1, triples]
    for first, after in zip(edges, edges[1:]):
        here = range(first, after)
        normed = [normed_ref[t // held, t % held * width : (t % held + 1) * width] for t in here]
        for k, p in enumerate(range(0, pairs, 4)):
            one = product([[l3_ref[t, p], normed[t - first]] for t in here], 3 * k)
            two = product([[l3_ref[t, p + 2], normed[t - first]] for t in here], 3 * k + 1)
            direct = product([[l3_ref[t, p + 1], l3_ref[t, p + 3]] for t in here], 3 * k + 2)
            if first == 0 and k == 0:
                fetch.wait()
            sums = [
                one[:, :width],
                one[:, width:] + direct[:, :width],
                two[:, :width],
                two[:, width:] + direct[:, width:],
            ]
            for t in here:
                for j in range(4):
                    mask = flags[p + j, t].astype(jnp.float32)
                    tile = sums[j][(t - first) * width : (t - first + 1) * width] * mask
                    out_ref[t, p + j] = tile.astype(jnp.bfloat16)
        for t in here:
            stores[t].start()
    for store in stores:
        store.wait()


def residual(turn, core, flags, l3, normed, weights, before=None, block=2):
    triples, pairs, width, _ = l3.shape

    def kernel(core_ref, *refs):
        refs = refs[:4] + refs[5:] if before is not None else refs

        @pl.when(core_ref[0] == turn)
        def _():
            final_kernel(core_ref, *refs, block=block)

    hbm = pl.BlockSpec(memory_space=pltpu.HBM)
    operands = [core, flags, l3, normed, weights]
    in_specs = [pl.BlockSpec(memory_space=pltpu.SMEM), hbm, *whole(3)]
    if before is not None:
        operands.append(before)
        in_specs.append(hbm)
    return pl.pallas_call(
        kernel,
        in_specs=in_specs,
        out_specs=hbm,
        out_shape=jax.ShapeDtypeStruct(l3.shape, jnp.bfloat16),
        input_output_aliases={} if before is None else {5: 0},
        scratch_shapes=[
            pltpu.VMEM(l3.shape, jnp.bfloat16),
            pltpu.SMEM(flags.shape, jnp.int32),
            pltpu.SemaphoreType.DMA,
            pltpu.SemaphoreType.DMA((triples,)),
        ],
        compiler_params=params(MEDIUM),
        cost_estimate=pl.CostEstimate(
            flops=4 * triples * pairs * width**3, bytes_accessed=l3.size * 4, transcendentals=0
        ),
        name="residual",
    )(*operands)


def own_indices():
    me = lax.axis_index(OCC).astype(jnp.uint32)
    return [me ^ jnp.uint32(step) for step in range(lax.axis_size(OCC))]


def occ_sum(blocks, indices):
    count = blocks.shape[0]
    zero = jnp.uint32(0)
    total = None
    for step in (0, 2, 3, 1):
        starts = (indices[step], *[zero] * (blocks.ndim - 1))
        block = lax.dynamic_slice(blocks, starts, (1, *blocks.shape[1:]))[0]
        if step:
            block = lax.ppermute(block, OCC, [(i, i ^ step) for i in range(count)])
        total = block if total is None else total + block
    return total


def halo(panels):
    count = lax.axis_size(VIR)
    ring = [((v, 0), ((v + 1) % count, 0)) for v in range(count)]
    ring += [((v, 1), ((v - 1) % count, 1)) for v in range(count)]
    pairs = [(2 * v + c, 2 * w + d) for (v, c), (w, d) in ring]
    mine = lax.ppermute(panels, (*VIR, "core"), pairs)
    other = lax.ppermute(mine, "core", [(0, 1), (1, 0)])
    first = lax.axis_index("core") == 0
    return jnp.where(first, mine, other), jnp.where(first, other, mine)


def shards(l3_tiles, active, panels, coupling):
    triples, pairs, width, _ = l3_tiles.shape
    vir_count, occ_count = lax.axis_size(VIR), lax.axis_size(OCC)
    near, far = lax.axis_size(NEAR), lax.axis_size("zh")
    rows = width // vir_count
    flags = active.T
    partial = partial_sums(flags, l3_tiles, panels)
    partial, sent = lax.optimization_barrier((partial, panels))
    before, after = halo(sent)
    parts = lax.all_to_all(partial.reshape(near, -1, width), NEAR, 0, 0, tiled=True)

    window = jnp.concatenate([before, panels, after], axis=0)
    flat_window = window.reshape(3 * pairs, width * width).astype(jnp.float32)
    combined = jnp.dot(coupling, flat_window, precision=lax.Precision.HIGHEST)
    combined = combined.reshape(pairs, width, width).astype(jnp.bfloat16)
    parts, combined = lax.optimization_barrier((parts, combined))

    part, combined = lax.optimization_barrier((near_sums(parts), combined))
    parts = [part]
    for step in (2, 3, 1):
        parts.append(lax.ppermute(part, "zh", [(i, i ^ step) for i in range(far)]))
    weights = stacked_weights(l3_tiles, combined, panels)
    line = lax.axis_index("zh").reshape(1)
    core = lax.axis_index("core").reshape(1)
    indices = own_indices()
    parts, weights, line, core, indices = lax.optimization_barrier(
        (parts, weights, line, core, indices)
    )

    copies = normed_copies(parts, line, rows, near)
    gathered = lax.all_to_all(copies, NEAR, 0, 0, tiled=True)
    high_low = gathered[:, -EXTRA:][:, : 2 * triples // near * rows].astype(jnp.float32)
    high_low = high_low.reshape(near, 2, triples // near, rows, width)
    local = (high_low[:, 0] + high_low[:, 1]).reshape(occ_count, triples // occ_count, rows, width)
    r3_tiles = residual(1, core, flags, l3_tiles, gathered, weights)
    local, r3_tiles = lax.optimization_barrier((local, r3_tiles))
    total = occ_sum(local, indices)
    r3_tiles = residual(0, core, flags, l3_tiles, gathered, weights, r3_tiles)
    l2_block = (total / jnp.sqrt(jnp.float32(pairs * vir_count))).astype(jnp.bfloat16)
    return (r3_tiles, l2_block)


def solution(mesh):
    vir_count, occ_count = mesh.devices.shape
    split = mesh.devices.reshape(2, 4, vir_count // 16, 2, occ_count // 2, 2)
    return jax.shard_map(
        shards,
        mesh=Mesh(split, (*VIR, *OCC)),
        in_specs=(
            P(OCC, VIR, None, None),
            P(OCC, VIR),
            P(VIR, None, None),
            P(VIR, None),
        ),
        out_specs=(P(OCC, VIR, None, None), P(OCC, VIR, None)),
        check_vma=False,
    )
```
